128 devices in a mesh: gx: 8 (over y, core), gy: 16 (over x, z).
Axes of the slice: x: 4, y: 4, z: 4, core: 2. Of those that a mesh axis runs over, the one named last changes fastest.
Arguments:
- fine_rhs: float32 [131072], P(('gx', 'gy')), may hold values from -30 to 30
- fine_diagonal: float32 [131072], P(('gx', 'gy')), may hold values from 0.25 to 2
- fine_support: int32 [27, 131072], P(None, ('gx', 'gy')), may hold values from -1 to 2048, as said below
- fine_weights: float32 [27, 131072], P(None, ('gx', 'gy')), may hold values from -0.2 to 0.2
- point_inputs: bfloat16 [32, 524288], P(None, ('gx', 'gy')), may hold values from -6 to 6
- point_offsets: float32 [3, 524288], P(None, ('gx', 'gy')), may hold values from 0 to 1
- point_counts: int32 [32768], P(('gx', 'gy')), may hold values from 0 to 16
- coarse_features: bfloat16 [32, 32768], P(None, ('gx', 'gy')), may hold values from -6 to 6
- coarse_support: int32 [27, 32768], P(None, ('gx', 'gy')), may hold values from -1 to 767, as said below
- w_first: bfloat16 [32, 64], replicated, may hold values from -1 to 1
- w_second: bfloat16 [64, 32], replicated, may hold values from -0.75 to 0.75
Outputs:
- solution_fine: float32 [131072], P(('gx', 'gy'))
- residual_fine: float32 [131072], P(('gx', 'gy'))
- gram: bfloat16 [27, 27, 32768], P(None, None, ('gx', 'gy'))
The draws below stay inside these ranges and needn't reach their ends.
Inputs may be any that keep to these rules, and one draw needn't show every extreme that they name: `fine_support`: every live entry of column u names a fine voxel u + value - 1024 inside the grid. `coarse_support`: every live entry of column v names a coarse voxel of the block just before v's block, v's own or the one just after (256 voxels a block), inside the grid.
All inputs are finite; a program needn't handle non-finite values.
Results may differ from the reference program's by a relative error of at most 0.0054.
Values may be sent and summed in bfloat16 or wider, within the bound.
A program may use at most 64 MiB of HBM per device.

```python
import math
import jax
import jax.numpy as jnp
from jax import lax

COARSE_DEV = 256
SLOTS = 16
WIDTH = 32
MLP_WIDTH = 64
SUPPORT = 27
ITERS = 2
REACH = 1024
FINE_TOT = 131072
COARSE_TOT = 32768
POINT_TOT = 524288
N_GX = 8
N_GY = 16


def draw_fine_support(key, part):
    key = jax.random.fold_in(key, 11)
    first, second = jax.random.split(key)
    column = jnp.arange(FINE_TOT, dtype=jnp.int32)
    offset = jax.random.randint(first, (SUPPORT, FINE_TOT), -REACH, REACH + 1)
    target = column[None, :] + offset
    offset = jnp.where((target < 0) | (target >= FINE_TOT), 0, offset)
    value = offset + REACH
    value = jnp.where(jax.random.randint(second, (SUPPORT, FINE_TOT), 0, 9) == 0, -1, value)
    value = value.at[0, 0].set(2 * REACH)
    return value.at[SUPPORT - 1, 0].set(-1).astype(jnp.int32)


def draw_coarse_support(key, part):
    key = jax.random.fold_in(key, 12)
    first, second, third = jax.random.split(key, 3)
    column = jnp.arange(COARSE_TOT, dtype=jnp.int32)
    owner = column // COARSE_DEV
    owners = COARSE_TOT // COARSE_DEV
    pick = jax.random.randint(first, (SUPPORT, COARSE_TOT), 0, 8)
    step = jnp.where(pick == 0, -1, jnp.where(pick == 1, 1, 0))
    target = owner[None, :] + step
    step = jnp.where((target < 0) | (target >= owners), 0, step)
    value = (step + 1) * COARSE_DEV + jax.random.randint(second, (SUPPORT, COARSE_TOT), 0, COARSE_DEV)
    value = jnp.where(jax.random.randint(third, (SUPPORT, COARSE_TOT), 0, 9) == 0, -1, value)
    value = value.at[0, 0].set(3 * COARSE_DEV - 1)
    return value.at[SUPPORT - 1, 0].set(-1).astype(jnp.int32)


def draw_point_counts(key, part):
    key = jax.random.fold_in(key, 13)
    first, second = jax.random.split(key)
    voxel = jnp.arange(COARSE_TOT, dtype=jnp.int32)
    level = jax.random.randint(first, (COARSE_TOT // COARSE_DEV,), 1, 5)
    counts = jax.random.randint(second, (COARSE_TOT,), 0, SLOTS + 1) * level[voxel // COARSE_DEV] // 4
    counts = jnp.where(voxel % COARSE_DEV == 0, SLOTS, counts)
    return counts.astype(jnp.int32)


def draw_fine_rhs(key, part):
    key = jax.random.fold_in(key, 14)
    first, second = jax.random.split(key)
    place = jnp.arange(FINE_TOT, dtype=jnp.float32) / FINE_TOT
    ramp = 1.0 + 2.0 * place
    spread = jnp.exp(jax.random.uniform(first, (FINE_TOT,), jnp.float32, math.log(0.3), math.log(3.0)))
    value = jax.random.normal(second, (FINE_TOT,), jnp.float32) * spread * ramp
    return jnp.clip(value, -30.0, 30.0)


def levels(key, dims, cuts, least, high):
    factor_of, own = 1.0, jax.random.fold_in(key, 6)
    for dim, blocks in cuts:
        heights = jnp.exp(jax.random.uniform(jax.random.fold_in(own, dim), (blocks,), jnp.float32, least / len(cuts), high / len(cuts)))
        factor_of = factor_of * jnp.repeat(heights, dims[dim] // blocks).reshape([-1 if axis == dim else 1 for axis in range(len(dims))])
    return factor_of


def noise(own_key, shape, deviation, reach, pieces=(), held_as=jnp.bfloat16):
    drawn = jax.random.normal(own_key, shape, jnp.float32) * deviation
    if len(pieces) > 0:
        drawn = levels(own_key, shape, pieces, -0.22, 0.18) * drawn
    return jnp.clip(drawn, min=-reach, max=reach).astype(held_as)


def setup_inputs(seed: int = 0) -> dict:
    streams_of = jax.random.split(jax.random.key(seed), 12)
    fine_rhs = draw_fine_rhs(jax.random.fold_in(streams_of[11], 71), 0)
    fine_diagonal = jnp.clip(0.25 + 1.75 * jax.random.uniform(streams_of[1], (FINE_TOT,), jnp.float32) ** levels(streams_of[1], (FINE_TOT,), ((0, 128),), -0.2, 0.2), 0.25, 2.0)
    fine_support = draw_fine_support(jax.random.fold_in(streams_of[11], 71), 0)
    fine_weights = jnp.clip(jax.random.uniform(streams_of[3], (SUPPORT, FINE_TOT), jnp.float32, -0.2, 0.2) * levels(streams_of[3], (SUPPORT, FINE_TOT), ((1, 128),), -0.4, 0.0), -0.2, 0.2)
    point_inputs = noise(streams_of[4], (WIDTH, POINT_TOT), 1.0, 6.0, ((1, 128),))
    point_offsets = jnp.clip(1.0 * jax.random.uniform(streams_of[5], (3, POINT_TOT), jnp.float32) ** levels(streams_of[5], (3, POINT_TOT), ((1, 128),), -0.2, 0.2), 0.0, 1.0)
    point_counts = draw_point_counts(jax.random.fold_in(streams_of[11], 71), 0)
    coarse_features = noise(streams_of[7], (WIDTH, COARSE_TOT), 1.0, 6.0, ((1, 128),))
    coarse_support = draw_coarse_support(jax.random.fold_in(streams_of[11], 71), 0)
    w_first = noise(streams_of[9], (WIDTH, MLP_WIDTH), WIDTH ** -0.5, 1.0)
    w_second = noise(streams_of[10], (MLP_WIDTH, WIDTH), MLP_WIDTH ** -0.5, 0.75)
    return {"fine_rhs": fine_rhs, "fine_diagonal": fine_diagonal, "fine_support": fine_support, "fine_weights": fine_weights, "point_inputs": point_inputs, "point_offsets": point_offsets, "point_counts": point_counts, "coarse_features": coarse_features, "coarse_support": coarse_support, "w_first": w_first, "w_second": w_second}


def fine_terms(vec, support, weights):
    column = jnp.arange(vec.shape[0], dtype=jnp.int32)

    def add_entry(carry, row):
        index, weight = row
        target = column + index.astype(jnp.int32) - REACH
        safe = jnp.clip(target, 0, vec.shape[0] - 1).astype(jnp.int32)
        live = jnp.where(index >= 0, weight, jnp.zeros_like(weight))
        forward, backward = carry
        forward = forward + live * vec[safe]
        backward = backward.at[safe].add(live * vec)
        return (forward, backward), None
    start = (jnp.zeros_like(vec), jnp.zeros_like(vec))
    (forward, backward), _ = lax.scan(add_entry, start, (support, weights))
    return forward, backward


def reference(fine_rhs, fine_diagonal, fine_support, fine_weights, point_inputs, point_offsets, point_counts, coarse_features, coarse_support, w_first, w_second):
    live_w = jnp.where(fine_support >= 0, fine_weights, jnp.zeros_like(fine_weights))
    row_abs = jnp.sum(jnp.abs(live_w), axis=0)
    _, col_abs = fine_terms(jnp.ones_like(fine_rhs), fine_support, jnp.abs(live_w))
    shift = fine_diagonal + row_abs + col_abs

    def operate(vec):
        forward, backward = fine_terms(vec, fine_support, live_w)
        return shift * vec + forward + backward

    solution_fine = jnp.zeros_like(fine_rhs)
    residual_fine = fine_rhs
    direction = fine_rhs
    norm_now = jnp.sum(residual_fine * residual_fine)
    for step in range(ITERS):
        image = operate(direction)
        alpha = norm_now / jnp.sum(direction * image)
        solution_fine = solution_fine + alpha * direction
        residual_fine = residual_fine - alpha * image
        norm_next = jnp.sum(residual_fine * residual_fine)
        direction = residual_fine + (norm_next / norm_now) * direction
        norm_now = norm_next

    point_hidden = jax.nn.relu(jnp.einsum("ei,ep->ip", w_first.astype(jnp.float32), point_inputs.astype(jnp.float32))).astype(jnp.bfloat16)
    point_feats = jnp.einsum("ie,ip->ep", w_second.astype(jnp.float32), point_hidden.astype(jnp.float32)).astype(jnp.bfloat16)
    blocks = N_GX * N_GY

    def regroup(table):
        rows = table.shape[0]
        table = table.reshape(rows, blocks, SLOTS, COARSE_DEV)
        return jnp.transpose(table, (0, 2, 1, 3)).reshape(rows, SLOTS, blocks * COARSE_DEV)

    feats = regroup(point_feats).astype(jnp.float32)
    offsets = regroup(point_offsets)
    live = (jnp.arange(SLOTS, dtype=jnp.int32)[:, None] < point_counts[None, :]).astype(jnp.float32)
    basis = jnp.stack([0.5 * (1.0 - offsets) ** 2, 0.5 + offsets - offsets * offsets, 0.5 * offsets * offsets])
    scale = WIDTH ** -0.5
    voxel_base = (jnp.arange(COARSE_TOT, dtype=jnp.int32) // COARSE_DEV - 1) * COARSE_DEV

    def one_entry(args):
        index, place = args
        valid = (index >= 0).astype(jnp.float32)
        target = jnp.clip(voxel_base + index.astype(jnp.int32), 0, COARSE_TOT - 1).astype(jnp.int32)
        near = coarse_features[:, target].astype(jnp.float32)
        dots = jnp.einsum("esc,ec->sc", feats, near)
        bezier = basis[place // 9, 0] * basis[(place // 3) % 3, 1] * basis[place % 3, 2]
        return dots * scale * bezier * live * valid[None, :]

    kernel = lax.map(one_entry, (coarse_support, jnp.arange(SUPPORT, dtype=jnp.int32)))

    def one_row(row):
        return jnp.sum(row[None] * kernel, axis=1).astype(jnp.bfloat16)

    gram = lax.map(one_row, kernel)
    return solution_fine, residual_fine, gram
```

```python
import functools

import jax
import jax.numpy as jnp
from jax import lax
from jax.experimental import pallas as pl
from jax.experimental.pallas import tpu as pltpu
from jax.sharding import PartitionSpec as P

MESH = pl.DeviceIdType.MESH
F32 = jnp.float32
BF16 = jnp.bfloat16
SUPPORT = 27
LANES = 128
ROWS = 8
CLASSES = 17
WINDOW = 24
SLOTS = 16
WIDTH = 32
HIDDEN = 64
COARSE = 256
POINTS = 4096
NT = (((1,), (1,)), ((), ()))
TN = (((0,), (0,)), ((), ()))


def spread_rows(row, shape):
    return jnp.broadcast_to(row, shape)


def kernel(
    n_gx,
    n_gy,
    rhs, rhs_row, diag, sup, wts, pin, off, cnt, cf, cs, w1, w2,
    sol_o, res_o, gram_o,
    row0, diag_v, sup_v, wts_v, pin_v, off_v, cnt_v, cs_v, w1_v, w2_v,
    hi_s, lo_s, lw_s, xw0, xw1, row1, fwd, quad, rabs, q0_s, shift_s, sol_v, res_v, mid0, mid1,
    sp_out0, sp_in0, sp_out1, sp_in1,
    ag, agx,
    cfw, fwin, feats, near, kern, gram_v,
    in_sem, halo_send, halo_recv, cf_send, cf_recv, sp_send, sp_recv,
    ag_send, ag_recv, agx_send, agx_recv, out_sem,
):
    gx = lax.axis_index("gx")
    gy = lax.axis_index("gy")
    n = n_gx * n_gy
    block = gx * n_gy + gy
    right_b = lax.rem(block + 1, n)
    left_b = lax.rem(block + n - 1, n)
    right = (lax.div(right_b, n_gy), lax.rem(right_b, n_gy))
    left = (lax.div(left_b, n_gy), lax.rem(left_b, n_gy))

    moves = [
        (sup, sup_v), (wts, wts_v), (rhs, xw0.at[pl.ds(8, 8)]), (rhs_row, row0), (cf, cfw.at[1]), (diag, diag_v),
        (pin, pin_v), (w1, w1_v), (w2, w2_v), (cs, cs_v), (off, off_v), (cnt, cnt_v),
    ]
    copies = [pltpu.make_async_copy(src, dst, in_sem.at[i]) for i, (src, dst) in enumerate(moves)]
    for copy in copies:
        copy.start()

    barrier = pltpu.get_barrier_semaphore()
    pl.semaphore_signal(barrier, inc=1, device_id=left, device_id_type=MESH)
    pl.semaphore_signal(barrier, inc=1, device_id=right, device_id_type=MESH)
    for d in range(1, n_gy):
        pl.semaphore_signal(barrier, inc=1, device_id=(gx, lax.rem(gy + d, n_gy)), device_id_type=MESH)
    for d in range(1, n_gx):
        pl.semaphore_signal(barrier, inc=1, device_id=(lax.rem(gx + d, n_gx), gy), device_id_type=MESH)

    def remote(src, dst, send, recv, device):
        return pltpu.make_async_remote_copy(
            src_ref=src, dst_ref=dst, send_sem=send, recv_sem=recv, device_id=device, device_id_type=MESH
        )

    copies[0].wait()
    copies[1].wait()
    lane = lax.broadcasted_iota(jnp.int32, (8, LANES), 1)
    for b in range(4):
        rows = 8 if b < 3 else 3
        for r in range(ROWS):
            at = (slice(8 * b, 8 * b + rows), slice(LANES * r, LANES * (r + 1)))
            value = sup_v[at]
            place = value + lane[:rows]
            live = jnp.where(value >= 0, wts_v[at], 0.0)
            hi = lax.shift_right_arithmetic(place, 7)
            lo = jnp.bitwise_and(place, 127)
            if rows < 8:
                pad = 8 - rows
                at = (slice(8 * b, 8 * b + 8), at[1])
                hi = jnp.concatenate([hi, jnp.full((pad, LANES), -1, jnp.int32)], axis=0)
                lo = jnp.concatenate([lo, jnp.zeros((pad, LANES), jnp.int32)], axis=0)
                live = jnp.concatenate([live, jnp.zeros((pad, LANES), F32)], axis=0)
            hi_s[at] = hi
            lo_s[at] = lo
            lw_s[at] = live

    for i in (2, 3, 4, 5):
        copies[i].wait()
    pl.semaphore_wait(barrier, 2 + (n_gy - 1) + (n_gx - 1))

    def halo(window, k):
        return [
            remote(window.at[pl.ds(8, 8)], window.at[pl.ds(0, 8)], halo_send.at[k, 0], halo_recv.at[k, 0], right),
            remote(window.at[pl.ds(8, 8)], window.at[pl.ds(16, 8)], halo_send.at[k, 1], halo_recv.at[k, 1], left),
        ]

    halo0 = halo(xw0, 0)
    for copy in halo0:
        copy.start()
    cf_halo = [
        remote(cfw.at[1], cfw.at[0], cf_send.at[0], cf_recv.at[0], right),
        remote(cfw.at[1], cfw.at[2], cf_send.at[1], cf_recv.at[1], left),
    ]
    for copy in cf_halo:
        copy.start()

    iota_hi = lax.broadcasted_iota(jnp.int32, (WINDOW, LANES), 0)
    iota_lo = lax.broadcasted_iota(jnp.int32, (LANES, LANES), 0)

    def two_terms(value):
        first = value.astype(BF16).astype(F32)
        return [first, value - first]

    def scatter(field_row, with_abs):
        count = 4 if with_abs else 2

        def step(j, total):
            hi = hi_s[pl.ds(j, 1), :]
            lo = lo_s[pl.ds(j, 1), :]
            w = lw_s[pl.ds(j, 1), :]
            terms = two_terms(w * field_row[...])
            if with_abs:
                terms = terms + two_terms(jnp.abs(w))
            left_parts, ones = [], []
            for r in range(ROWS):
                at = slice(LANES * r, LANES * (r + 1))
                hit = spread_rows(hi[:, at], (WINDOW, LANES)) == iota_hi - r
                left_parts.append(
                    jnp.concatenate(
                        [jnp.where(hit, spread_rows(t[:, at], (WINDOW, LANES)), 0.0) for t in terms], axis=0
                    ).astype(BF16)
                )
                ones.append(
                    jnp.where(spread_rows(lo[:, at], (LANES, LANES)) == iota_lo, 1.0, 0.0).astype(BF16)
                )
            return total + lax.dot_general(
                jnp.concatenate(left_parts, axis=1), jnp.concatenate(ones, axis=1), NT, preferred_element_type=F32
            )

        total = lax.fori_loop(0, SUPPORT, step, jnp.zeros((WINDOW * count, LANES), F32))
        out = [total[:24] + total[24:48]]
        if with_abs:
            out.append(total[48:72] + total[72:96])
        return out

    def send_spread(parts, out, into, k):
        for i, part in enumerate(parts):
            out[0, 8 * i : 8 * i + 8, :] = part[0:8]
            out[1, 8 * i : 8 * i + 8, :] = part[16:24]
        copies = [
            remote(out.at[0], into.at[0], sp_send.at[k, 0], sp_recv.at[k, 0], left),
            remote(out.at[1], into.at[1], sp_send.at[k, 1], sp_recv.at[k, 1], right),
        ]
        for copy in copies:
            copy.start()
        return copies

    def forward(window, with_abs):
        def row(r, carry):
            near_rows = [spread_rows(window[pl.ds(r + k, 1), :], (8, LANES)) for k in range(CLASSES)]
            lanes = pl.ds(pl.multiple_of(r * LANES, LANES), LANES)
            total = jnp.zeros((8, LANES), F32)
            squares = jnp.zeros((8, LANES), F32)
            weight = jnp.zeros((8, LANES), F32)
            for b in range(4):
                hi = hi_s[8 * b : 8 * b + 8, lanes]
                lo = lo_s[8 * b : 8 * b + 8, lanes]
                w = lw_s[8 * b : 8 * b + 8, lanes]
                got = jnp.zeros((8, LANES), F32)
                for k in range(CLASSES):
                    got = jnp.where(hi == k, jnp.take_along_axis(near_rows[k], lo, axis=1, mode="promise_in_bounds"), got)
                total = total + w * got
                if with_abs:
                    size = jnp.abs(w)
                    squares = squares + size * (got * got)
                    weight = weight + size
            fwd[pl.ds(r, 1), :] = jnp.sum(total, axis=0, keepdims=True)
            if with_abs:
                quad[pl.ds(r, 1), :] = jnp.sum(squares, axis=0, keepdims=True)
                rabs[pl.ds(r, 1), :] = jnp.sum(weight, axis=0, keepdims=True)
            return carry

        lax.fori_loop(0, ROWS, row, 0)

    def gather_first(k, tile):
        ag[k, gy] = tile
        copies = []
        for d in range(1, n_gy):
            copies.append(
                remote(ag.at[k, gy], ag.at[k, gy], ag_send.at[k, d], ag_recv.at[k, d], (gx, lax.rem(gy + d, n_gy)))
            )
            copies[-1].start()
        return copies

    def gather_second(k, copies):
        for copy in copies:
            copy.wait()
        agx[k, gx] = jnp.sum(ag[k], axis=0)
        copies = []
        for d in range(1, n_gx):
            copies.append(
                remote(agx.at[k, gx], agx.at[k, gx], agx_send.at[k, d], agx_recv.at[k, d], (lax.rem(gx + d, n_gx), gy))
            )
            copies[-1].start()
        return copies

    def gather_end(k, copies):
        for copy in copies:
            copy.wait()
        total = jnp.sum(jnp.sum(agx[k], axis=0), axis=1, keepdims=True)
        return total[0:1], total[1:2]

    def tile_of(first, second):
        return jnp.concatenate(
            [
                jnp.sum(first, axis=0, keepdims=True),
                jnp.sum(second, axis=0, keepdims=True),
                jnp.zeros((6, LANES), F32),
            ],
            axis=0,
        )

    def split_off(parts, out, into, k, keep):
        for i, part in enumerate(parts):
            keep[8 * i : 8 * i + 8, :] = part[8:16]
        return send_spread(parts, out, into, k)

    spread0 = split_off(scatter(row0, True), sp_out0, sp_in0, 0, mid0)
    for copy in halo0:
        copy.wait()
    forward(xw0, True)
    r0 = xw0[8:16, :]
    first0 = gather_first(
        0, tile_of(r0 * r0, (diag_v[...] + rabs[...]) * (r0 * r0) + quad[...] + 2.0 * r0 * fwd[...])
    )

    for i in range(6, 12):
        copies[i].wait()

    chunk = 512

    def mlp(i, carry):
        at = pl.ds(pl.multiple_of(i * chunk, chunk), chunk)
        hidden = lax.dot_general(w1_v[...], pin_v[:, at], TN, preferred_element_type=F32)
        hidden = jnp.maximum(hidden, 0.0).astype(BF16)
        out = lax.dot_general(w2_v[...], hidden, TN, preferred_element_type=F32)
        feats[:, at] = out.astype(BF16).astype(F32)
        return carry

    lax.fori_loop(0, POINTS // chunk, mlp, 0)
    second0 = gather_second(0, first0)

    for copy in cf_halo:
        copy.wait()
    for side in range(3):
        fwin[:, COARSE * side : COARSE * (side + 1)] = cfw[side].astype(F32)

    def support_features(e, carry):
        line = fwin[pl.ds(e, 1), :]
        sources = [spread_rows(line[:, LANES * k : LANES * (k + 1)], (8, LANES)) for k in range(6)]
        for c in range(2):
            for b in range(4):
                rows = 8 if b < 3 else 3
                value = cs_v[8 * b : 8 * b + rows, LANES * c : LANES * (c + 1)]
                if rows < 8:
                    value = jnp.concatenate([value, jnp.full((8 - rows, LANES), -1, jnp.int32)], axis=0)
                hi = lax.shift_right_arithmetic(value, 7)
                lo = jnp.bitwise_and(value, 127)
                got = jnp.zeros((8, LANES), F32)
                for k in range(6):
                    got = jnp.where(hi == k, jnp.take_along_axis(sources[k], lo, axis=1, mode="promise_in_bounds"), got)
                near[c, e, 8 * b : 8 * b + 8, :] = got
        return carry

    lax.fori_loop(0, WIDTH, support_features, 0)

    rr0, dad0 = gather_end(0, second0)
    alpha0 = rr0 / dad0
    for copy in spread0:
        copy.wait()
    shift_s[...] = diag_v[...] + rabs[...] + (mid0[8:16, :] + sp_in0[0, 8:16, :] + sp_in0[1, 8:16, :])
    q0_s[...] = shift_s[...] * r0 + fwd[...] + (mid0[0:8, :] + sp_in0[0, 0:8, :] + sp_in0[1, 0:8, :])
    r1 = r0 - alpha0 * q0_s[...]
    xw1[8:16, :] = r1
    halo1 = halo(xw1, 1)
    for copy in halo1:
        copy.start()
    for r in range(ROWS):
        row1[0:1, LANES * r : LANES * (r + 1)] = r1[r : r + 1]

    spread1 = split_off(scatter(row1, False), sp_out1, sp_in1, 1, mid1)
    for copy in halo1:
        copy.wait()
    forward(xw1, False)
    r1 = xw1[8:16, :]
    first1 = gather_first(1, tile_of(r1 * r1, shift_s[...] * (r1 * r1) + 2.0 * r1 * fwd[...]))

    iota_j = lax.broadcasted_iota(jnp.int32, (32, LANES), 0)
    digit = [lax.div(iota_j, 9), lax.rem(lax.div(iota_j, 3), 3), lax.rem(iota_j, 3)]
    group = 4

    def kernel_values(i, carry):
        c = lax.rem(i, 2)
        s0 = lax.div(i, 2) * group
        points = [pl.ds(pl.multiple_of((s0 + g) * COARSE + c * LANES, LANES), LANES) for g in range(group)]
        dots = [[jnp.zeros((8, LANES), F32) for _ in range(4)] for _ in range(group)]
        for e in range(WIDTH):
            sources = [near[c, e, 8 * b : 8 * b + 8, :] for b in range(4)]
            for g in range(group):
                feat = spread_rows(feats[e : e + 1, points[g]], (8, LANES))
                dots[g] = [dots[g][b] + feat * sources[b] for b in range(4)]
        counts = cnt_v[pl.ds(c, 1), :]
        for g in range(group):
            factor = jnp.where(s0 + g < counts, WIDTH**-0.5, 0.0)
            product = None
            for a in range(3):
                t = off_v[a : a + 1, points[g]]
                q = [0.5 * (1.0 - t) * (1.0 - t), 0.5 + t - t * t, 0.5 * t * t]
                if a == 0:
                    q = [part * factor for part in q]
                q = [spread_rows(part, (32, LANES)) for part in q]
                value = jnp.where(digit[a] == 0, q[0], jnp.where(digit[a] == 1, q[1], q[2]))
                product = value if product is None else product * value
            for b in range(4):
                kern[c, s0 + g, 8 * b : 8 * b + 8, :] = dots[g][b] * product[8 * b : 8 * b + 8]
        return carry

    lax.fori_loop(0, 2 * SLOTS // group, kernel_values, 0)
    second1 = gather_second(1, first1)

    def gram_rows(i, carry):
        c = lax.rem(i, 2)
        j0 = lax.div(i, 2) * 3
        here = pl.ds(pl.multiple_of(c * LANES, LANES), LANES)
        sums = [[jnp.zeros((8, LANES), F32) for _ in range(4)] for _ in range(3)]
        for s in range(SLOTS):
            columns = [kern[c, s, 8 * b : 8 * b + 8, :] for b in range(4)]
            for g in range(3):
                one = spread_rows(kern[c, s, pl.ds(j0 + g, 1), :], (8, LANES))
                sums[g] = [sums[g][b] + one * columns[b] for b in range(4)]
        for g in range(3):
            whole = jnp.concatenate(sums[g], axis=0).astype(BF16)
            gram_v[j0 + g, :, here] = whole[:SUPPORT]
        return carry

    lax.fori_loop(0, 18, gram_rows, 0)
    out2 = pltpu.make_async_copy(gram_v, gram_o, out_sem.at[2])
    out2.start()

    rr1, rar1 = gather_end(1, second1)
    beta = rr1 / rr0
    alpha1 = rr1 / (rar1 - beta * rr1 / alpha0)
    for copy in spread1:
        copy.wait()
    image = shift_s[...] * r1 + fwd[...] + (mid1[...] + sp_in1[0] + sp_in1[1])
    sol_v[...] = alpha0 * r0 + alpha1 * (r1 + beta * r0)
    res_v[...] = r1 - alpha1 * (image + beta * q0_s[...])
    out0 = pltpu.make_async_copy(sol_v, sol_o, out_sem.at[0])
    out1 = pltpu.make_async_copy(res_v, res_o, out_sem.at[1])
    out0.start()
    out1.start()
    out0.wait()
    out1.wait()
    out2.wait()


def on_device(n_gx, n_gy, rhs, diag, sup, wts, pin, off, cnt, cf, cs, w1, w2):
    vm = pltpu.VMEM
    dma = pltpu.SemaphoreType.DMA
    fine = (ROWS, LANES)
    sol, res, gram = pl.pallas_call(
        functools.partial(kernel, n_gx, n_gy),
        out_shape=[
            jax.ShapeDtypeStruct(fine, F32),
            jax.ShapeDtypeStruct(fine, F32),
            jax.ShapeDtypeStruct((SUPPORT, SUPPORT, COARSE), BF16),
        ],
        in_specs=[pl.BlockSpec(memory_space=pl.ANY)] * 12,
        out_specs=[pl.BlockSpec(memory_space=pl.ANY)] * 3,
        scratch_shapes=[
            vm((1, 1024), F32),
            vm(fine, F32),
            vm((SUPPORT, 1024), jnp.int32),
            vm((SUPPORT, 1024), F32),
            vm((WIDTH, POINTS), BF16),
            vm((3, POINTS), F32),
            vm((2, LANES), jnp.int32),
            vm((SUPPORT, COARSE), jnp.int32),
            vm((WIDTH, HIDDEN), BF16),
            vm((HIDDEN, WIDTH), BF16),
            vm((32, 1024), jnp.int32),
            vm((32, 1024), jnp.int32),
            vm((32, 1024), F32),
            vm((WINDOW, LANES), F32),
            vm((WINDOW, LANES), F32),
            vm((1, 1024), F32),
            vm(fine, F32),
            vm(fine, F32),
            vm(fine, F32),
            vm(fine, F32),
            vm(fine, F32),
            vm(fine, F32),
            vm(fine, F32),
            vm((16, LANES), F32),
            vm((8, LANES), F32),
            vm((2, 16, LANES), F32),
            vm((2, 16, LANES), F32),
            vm((2, 8, LANES), F32),
            vm((2, 8, LANES), F32),
            vm((2, n_gy, 8, LANES), F32),
            vm((2, n_gx, 8, LANES), F32),
            vm((3, WIDTH, COARSE), BF16),
            vm((WIDTH, 3 * COARSE), F32),
            vm((WIDTH, POINTS), F32),
            vm((2, WIDTH, 32, LANES), F32),
            vm((2, SLOTS, 32, LANES), F32),
            vm((SUPPORT, SUPPORT, COARSE), BF16),
            dma((12,)),
            dma((2, 2)),
            dma((2, 2)),
            dma((2,)),
            dma((2,)),
            dma((2, 2)),
            dma((2, 2)),
            dma((2, n_gy)),
            dma((2, n_gy)),
            dma((2, n_gx)),
            dma((2, n_gx)),
            dma((3,)),
        ],
        compiler_params=pltpu.CompilerParams(
            collective_id=0, has_side_effects=True, vmem_limit_bytes=48 * 1024 * 1024
        ),
    )(
        rhs.reshape(fine), rhs.reshape(1, 1024), diag.reshape(fine), sup, wts, pin, off,
        cnt.reshape(2, LANES), cf, cs, w1, w2,
    )
    return sol.reshape(1024), res.reshape(1024), gram


def solution(mesh):
    both = ("gx", "gy")
    placed = (
        P(both), P(both), P(None, both), P(None, both), P(None, both), P(None, both),
        P(both), P(None, both), P(None, both), P(), P(),
    )
    return jax.shard_map(
        functools.partial(on_device, mesh.shape["gx"], mesh.shape["gy"]),
        mesh=mesh,
        in_specs=placed,
        out_specs=(P(both), P(both), P(None, None, both)),
        check_vma=False,
    )
```

```python
import functools

import jax
import jax.numpy as jnp
from jax import lax
from jax.experimental import pallas as pl
from jax.experimental.pallas import tpu as pltpu
from jax.sharding import PartitionSpec as P

MESH = pl.DeviceIdType.MESH
F32 = jnp.float32
BF16 = jnp.bfloat16
SUPPORT = 27
LANES = 128
ROWS = 8
CLASSES = 17
WINDOW = 24
SLOTS = 16
WIDTH = 32
HIDDEN = 64
COARSE = 256
POINTS = 4096
NT = (((1,), (1,)), ((), ()))
TN = (((0,), (0,)), ((), ()))


def spread_rows(row, shape):
    return jnp.broadcast_to(row, shape)


def kernel(
    n_gx,
    n_gy,
    rhs, rhs_row, diag, sup, wts, pin, off, cnt, cf, cs, w1, w2,
    sol_o, res_o, gram_o,
    row0, diag_v, sup_v, wts_v, pin_v, off_v, cnt_v, cs_v, w1_v, w2_v,
    hi_s, lo_s, lw_s, xw0, xw1, row1, fwd, rabs, shift_s, part, mid1, sol_v, res_v,
    to_left, to_right, from_left, from_right, to_left1, to_right1, from_left1, from_right1,
    ag, agx,
    cfw, fwin, feats, near, kern, gram_v,
    in_sem, halo_send, halo_recv, cf_send, cf_recv, ex_send, ex_recv,
    ag_send, ag_recv, agx_send, agx_recv, out_sem,
):
    gx = lax.axis_index("gx")
    gy = lax.axis_index("gy")
    n = n_gx * n_gy
    block = gx * n_gy + gy

    def device(step):
        other = lax.rem(block + n + step, n)
        return lax.div(other, n_gy), lax.rem(other, n_gy)

    left2, left, right, right2 = device(-2), device(-1), device(1), device(2)

    moves = [
        (rhs, xw0.at[pl.ds(8, 8)]), (cf, cfw.at[1]), (sup, sup_v), (wts, wts_v), (rhs_row, row0), (diag, diag_v),
        (pin, pin_v), (w1, w1_v), (w2, w2_v), (cs, cs_v), (off, off_v), (cnt, cnt_v),
    ]
    copies = [pltpu.make_async_copy(src, dst, in_sem.at[i]) for i, (src, dst) in enumerate(moves)]
    for copy in copies:
        copy.start()

    barrier = pltpu.get_barrier_semaphore()
    for other in (left, right, left2, right2):
        pl.semaphore_signal(barrier, inc=1, device_id=other, device_id_type=MESH)
    for d in range(1, n_gy):
        pl.semaphore_signal(barrier, inc=1, device_id=(gx, lax.rem(gy + d, n_gy)), device_id_type=MESH)
    for d in range(1, n_gx):
        pl.semaphore_signal(barrier, inc=1, device_id=(lax.rem(gx + d, n_gx), gy), device_id_type=MESH)

    def remote(src, dst, send, recv, device):
        return pltpu.make_async_remote_copy(
            src_ref=src, dst_ref=dst, send_sem=send, recv_sem=recv, device_id=device, device_id_type=MESH
        )

    for i in (0, 1):
        copies[i].wait()
    pl.semaphore_wait(barrier, 4 + (n_gy - 1) + (n_gx - 1))

    started = []

    def arrive(copies):
        for copy in copies:
            copy.wait_recv()
        started.extend(copies)

    halo0 = [
        remote(xw0.at[pl.ds(8, 8)], xw0.at[pl.ds(0, 8)], halo_send.at[0], halo_recv.at[0], right),
        remote(xw0.at[pl.ds(8, 8)], xw0.at[pl.ds(16, 8)], halo_send.at[1], halo_recv.at[1], left),
    ]
    for copy in halo0:
        copy.start()
    cf_halo = [
        remote(cfw.at[1], cfw.at[0], cf_send.at[0], cf_recv.at[0], right),
        remote(cfw.at[1], cfw.at[2], cf_send.at[1], cf_recv.at[1], left),
    ]
    for copy in cf_halo:
        copy.start()

    for i in range(2, 6):
        copies[i].wait()
    lane = lax.broadcasted_iota(jnp.int32, (8, LANES), 1)
    for b in range(4):
        rows = 8 if b < 3 else 3
        for r in range(ROWS):
            at = (slice(8 * b, 8 * b + rows), slice(LANES * r, LANES * (r + 1)))
            value = sup_v[at]
            place = value + lane[:rows]
            live = jnp.where(value >= 0, wts_v[at], 0.0)
            hi = lax.shift_right_arithmetic(place, 7)
            lo = jnp.bitwise_and(place, 127)
            if rows < 8:
                pad = 8 - rows
                at = (slice(8 * b, 8 * b + 8), at[1])
                hi = jnp.concatenate([hi, jnp.full((pad, LANES), -1, jnp.int32)], axis=0)
                lo = jnp.concatenate([lo, jnp.zeros((pad, LANES), jnp.int32)], axis=0)
                live = jnp.concatenate([live, jnp.zeros((pad, LANES), F32)], axis=0)
            hi_s[at] = hi
            lo_s[at] = lo
            lw_s[at] = live

    iota_hi = lax.broadcasted_iota(jnp.int32, (WINDOW, LANES), 0)
    iota_lo = lax.broadcasted_iota(jnp.int32, (LANES, LANES), 0)

    def two_terms(value):
        first = value.astype(BF16).astype(F32)
        return [first, value - first]

    def scatter(field_row, with_abs):
        count = 4 if with_abs else 2

        def step(j, total):
            hi = hi_s[pl.ds(j, 1), :]
            lo = lo_s[pl.ds(j, 1), :]
            w = lw_s[pl.ds(j, 1), :]
            terms = two_terms(w * field_row[...])
            if with_abs:
                terms = terms + two_terms(jnp.abs(w))
            left_parts, ones = [], []
            for r in range(ROWS):
                at = slice(LANES * r, LANES * (r + 1))
                hit = spread_rows(hi[:, at], (WINDOW, LANES)) == iota_hi - r
                left_parts.append(
                    jnp.concatenate(
                        [jnp.where(hit, spread_rows(t[:, at], (WINDOW, LANES)), 0.0) for t in terms], axis=0
                    ).astype(BF16)
                )
                ones.append(
                    jnp.where(spread_rows(lo[:, at], (LANES, LANES)) == iota_lo, 1.0, 0.0).astype(BF16)
                )
            return total + lax.dot_general(
                jnp.concatenate(left_parts, axis=1), jnp.concatenate(ones, axis=1), NT, preferred_element_type=F32
            )

        total = lax.fori_loop(0, SUPPORT, step, jnp.zeros((WINDOW * count, LANES), F32), unroll=9)
        out = [total[:24] + total[24:48]]
        if with_abs:
            out.append(total[48:72] + total[72:96])
        return out

    def forward(window, with_abs):
        def row(r, carry):
            near_rows = [spread_rows(window[pl.ds(r + k, 1), :], (8, LANES)) for k in range(CLASSES)]
            lanes = pl.ds(pl.multiple_of(r * LANES, LANES), LANES)
            total = jnp.zeros((8, LANES), F32)
            weight = jnp.zeros((8, LANES), F32)
            for b in range(4):
                hi = hi_s[8 * b : 8 * b + 8, lanes]
                lo = lo_s[8 * b : 8 * b + 8, lanes]
                w = lw_s[8 * b : 8 * b + 8, lanes]
                got = jnp.zeros((8, LANES), F32)
                for k in range(CLASSES):
                    got = jnp.where(hi == k, jnp.take_along_axis(near_rows[k], lo, axis=1, mode="promise_in_bounds"), got)
                total = total + w * got
                if with_abs:
                    weight = weight + jnp.abs(w)
            fwd[pl.ds(r, 1), :] = jnp.sum(total, axis=0, keepdims=True)
            if with_abs:
                rabs[pl.ds(r, 1), :] = jnp.sum(weight, axis=0, keepdims=True)
            return carry

        lax.fori_loop(0, ROWS, row, 0)

    def gather_first(tile):
        ag[gy] = tile
        copies = []
        for d in range(1, n_gy):
            copies.append(remote(ag.at[gy], ag.at[gy], ag_send.at[d], ag_recv.at[d], (gx, lax.rem(gy + d, n_gy))))
            copies[-1].start()
        return copies

    def gather_second(copies):
        arrive(copies)
        agx[gx] = jnp.sum(ag[...], axis=0)
        copies = []
        for d in range(1, n_gx):
            copies.append(remote(agx.at[gx], agx.at[gx], agx_send.at[d], agx_recv.at[d], (lax.rem(gx + d, n_gx), gy)))
            copies[-1].start()
        return copies

    def gather_end(copies):
        arrive(copies)
        total = jnp.sum(jnp.sum(agx[...], axis=0), axis=1, keepdims=True)
        return [total[i : i + 1] for i in range(4)]

    def tile_of(*fields):
        rows = [jnp.sum(field, axis=0, keepdims=True) for field in fields]
        return jnp.concatenate(rows + [jnp.zeros((8 - len(rows), LANES), F32)], axis=0)

    back, size = scatter(row0, True)
    arrive(halo0)
    forward(xw0, True)
    r0 = xw0[8:16, :]
    to_left[0:8, :] = back[0:8] + size[0:8] * xw0[0:8, :]
    to_left[8:16, :] = size[0:8]
    to_right[0:8, :] = back[16:24] + size[16:24] * xw0[16:24, :]
    to_right[8:16, :] = size[16:24]
    shift = diag_v[...] + rabs[...] + size[8:16]
    part[...] = shift * r0 + fwd[...] + back[8:16]
    shift_s[...] = shift
    near_by = [
        remote(part, from_left.at[pl.ds(0, 8)], ex_send.at[0], ex_recv.at[0], right),
        remote(part, from_right.at[pl.ds(0, 8)], ex_send.at[1], ex_recv.at[1], left),
        remote(to_right, from_left.at[pl.ds(8, 16)], ex_send.at[2], ex_recv.at[2], right),
        remote(to_left, from_right.at[pl.ds(8, 16)], ex_send.at[3], ex_recv.at[3], left),
        remote(to_right.at[pl.ds(0, 8)], from_left.at[pl.ds(24, 8)], ex_send.at[4], ex_recv.at[4], right2),
        remote(to_left.at[pl.ds(0, 8)], from_right.at[pl.ds(24, 8)], ex_send.at[5], ex_recv.at[5], left2),
    ]
    for copy in near_by:
        copy.start()

    for i in range(6, 12):
        copies[i].wait()

    chunk = 2048

    def mlp(i, carry):
        at = pl.ds(pl.multiple_of(i * chunk, chunk), chunk)
        hidden = lax.dot_general(w1_v[...], pin_v[:, at], TN, preferred_element_type=F32)
        hidden = jnp.maximum(hidden, 0.0).astype(BF16)
        out = jnp.dot(w2_v[...], hidden, preferred_element_type=F32)
        feats[:, at] = out.astype(BF16).astype(F32)
        return carry

    lax.fori_loop(0, POINTS // chunk, mlp, 0)

    arrive(cf_halo)
    for side in range(3):
        fwin[:, COARSE * side : COARSE * (side + 1)] = cfw[side].astype(F32)

    def support_features(e, carry):
        line = fwin[pl.ds(e, 1), :]
        sources = [spread_rows(line[:, LANES * k : LANES * (k + 1)], (8, LANES)) for k in range(6)]
        for c in range(2):
            for b in range(4):
                rows = 8 if b < 3 else 3
                value = cs_v[8 * b : 8 * b + rows, LANES * c : LANES * (c + 1)]
                if rows < 8:
                    value = jnp.concatenate([value, jnp.full((8 - rows, LANES), -1, jnp.int32)], axis=0)
                hi = lax.shift_right_arithmetic(value, 7)
                lo = jnp.bitwise_and(value, 127)
                got = jnp.zeros((8, LANES), F32)
                for k in range(6):
                    got = jnp.where(hi == k, jnp.take_along_axis(sources[k], lo, axis=1, mode="promise_in_bounds"), got)
                near[c, e, 8 * b : 8 * b + 8, :] = got
        return carry

    lax.fori_loop(0, WIDTH, support_features, 0, unroll=4)

    arrive(near_by)
    xw1[0:8, :] = from_left[0:8, :] + to_left[0:8, :] + from_left[24:32, :]
    xw1[8:16, :] = part[...] + from_left[8:16, :] + from_right[8:16, :]
    xw1[16:24, :] = from_right[0:8, :] + to_right[0:8, :] + from_right[24:32, :]
    shift_s[...] = shift_s[...] + (from_left[16:24, :] + from_right[16:24, :])
    forward(xw1, False)
    q0 = xw1[8:16, :]
    first = gather_first(tile_of(r0 * r0, r0 * q0, q0 * q0, shift_s[...] * (q0 * q0) + 2.0 * q0 * fwd[...]))
    for r in range(ROWS):
        row1[0:1, LANES * r : LANES * (r + 1)] = q0[r : r + 1]

    (back,) = scatter(row1, False)
    to_left1[...] = back[0:8]
    to_right1[...] = back[16:24]
    mid1[...] = back[8:16]
    ends = [
        remote(to_right1, from_left1, ex_send.at[6], ex_recv.at[6], right),
        remote(to_left1, from_right1, ex_send.at[7], ex_recv.at[7], left),
    ]
    for copy in ends:
        copy.start()

    iota_j = lax.broadcasted_iota(jnp.int32, (32, LANES), 0)
    digit = [lax.div(iota_j, 9), lax.rem(lax.div(iota_j, 3), 3), lax.rem(iota_j, 3)]
    group = 4

    def kernel_values(i, carry):
        c = lax.rem(i, 2)
        s0 = lax.div(i, 2) * group
        points = [pl.ds(pl.multiple_of((s0 + g) * COARSE + c * LANES, LANES), LANES) for g in range(group)]
        dots = [[jnp.zeros((8, LANES), F32) for _ in range(4)] for _ in range(group)]
        for e in range(WIDTH):
            sources = [near[c, e, 8 * b : 8 * b + 8, :] for b in range(4)]
            for g in range(group):
                feat = spread_rows(feats[e : e + 1, points[g]], (8, LANES))
                dots[g] = [dots[g][b] + feat * sources[b] for b in range(4)]
        counts = cnt_v[pl.ds(c, 1), :]
        for g in range(group):
            factor = jnp.where(s0 + g < counts, WIDTH**-0.5, 0.0)
            product = None
            for a in range(3):
                t = off_v[a : a + 1, points[g]]
                q = [0.5 * (1.0 - t) * (1.0 - t), 0.5 + t - t * t, 0.5 * t * t]
                if a == 0:
                    q = [part * factor for part in q]
                q = [spread_rows(part, (32, LANES)) for part in q]
                value = jnp.where(digit[a] == 0, q[0], jnp.where(digit[a] == 1, q[1], q[2]))
                product = value if product is None else product * value
            for b in range(4):
                kern[c, s0 + g, 8 * b : 8 * b + 8, :] = dots[g][b] * product[8 * b : 8 * b + 8]
        return carry

    lax.fori_loop(0, 2 * SLOTS // group, kernel_values, 0)
    second = gather_second(first)

    def gram_rows(i, carry):
        c = lax.rem(i, 2)
        j0 = lax.div(i, 2) * 3
        here = pl.ds(pl.multiple_of(c * LANES, LANES), LANES)
        sums = [[jnp.zeros((8, LANES), F32) for _ in range(4)] for _ in range(3)]
        for s in range(SLOTS):
            columns = [kern[c, s, 8 * b : 8 * b + 8, :] for b in range(4)]
            for g in range(3):
                one = spread_rows(kern[c, s, pl.ds(j0 + g, 1), :], (8, LANES))
                sums[g] = [sums[g][b] + one * columns[b] for b in range(4)]
        for g in range(3):
            whole = jnp.concatenate(sums[g], axis=0).astype(BF16)
            gram_v[j0 + g, :, here] = whole[:SUPPORT]
        return carry

    lax.fori_loop(0, 18, gram_rows, 0)
    out2 = pltpu.make_async_copy(gram_v, gram_o, out_sem.at[2])
    out2.start()

    rr0, rq, qq, qaq = gather_end(second)
    alpha0 = rr0 / rq
    shear = rq / rr0
    hh = qq - shear * rq
    hah = qaq - 2.0 * shear * qq + shear * shear * rq
    rr1 = alpha0 * alpha0 * hh
    beta = rr1 / rr0
    alpha1 = rr1 / (alpha0 * alpha0 * hah - beta * rr1 * shear)
    arrive(ends)
    r1 = r0 - alpha0 * q0
    image = shift_s[...] * q0 + fwd[...] + (mid1[...] + from_left1[...] + from_right1[...])
    sol_v[...] = alpha0 * r0 + alpha1 * (r1 + beta * r0)
    res_v[...] = r1 - alpha1 * ((1.0 + beta) * q0 - alpha0 * image)
    out0 = pltpu.make_async_copy(sol_v, sol_o, out_sem.at[0])
    out1 = pltpu.make_async_copy(res_v, res_o, out_sem.at[1])
    out0.start()
    out1.start()
    for copy in started:
        copy.wait_send()
    out0.wait()
    out1.wait()
    out2.wait()


def on_device(n_gx, n_gy, rhs, diag, sup, wts, pin, off, cnt, cf, cs, w1, w2):
    vm = pltpu.VMEM
    dma = pltpu.SemaphoreType.DMA
    fine = (ROWS, LANES)
    sol, res, gram = pl.pallas_call(
        functools.partial(kernel, n_gx, n_gy),
        out_shape=[
            jax.ShapeDtypeStruct(fine, F32),
            jax.ShapeDtypeStruct(fine, F32),
            jax.ShapeDtypeStruct((SUPPORT, SUPPORT, COARSE), BF16),
        ],
        in_specs=[pl.BlockSpec(memory_space=pl.ANY)] * 12,
        out_specs=[pl.BlockSpec(memory_space=pl.ANY)] * 3,
        scratch_shapes=[
            vm((1, 1024), F32),
            vm(fine, F32),
            vm((SUPPORT, 1024), jnp.int32),
            vm((SUPPORT, 1024), F32),
            vm((WIDTH, POINTS), BF16),
            vm((3, POINTS), F32),
            vm((2, LANES), jnp.int32),
            vm((SUPPORT, COARSE), jnp.int32),
            vm((WIDTH, HIDDEN), BF16),
            vm((WIDTH, HIDDEN), BF16),
            vm((32, 1024), jnp.int32),
            vm((32, 1024), jnp.int32),
            vm((32, 1024), F32),
            vm((WINDOW, LANES), F32),
            vm((WINDOW, LANES), F32),
            vm((1, 1024), F32),
            vm(fine, F32),
            vm(fine, F32),
            vm(fine, F32),
            vm(fine, F32),
            vm(fine, F32),
            vm(fine, F32),
            vm(fine, F32),
            vm((16, LANES), F32),
            vm((16, LANES), F32),
            vm((32, LANES), F32),
            vm((32, LANES), F32),
            vm(fine, F32),
            vm(fine, F32),
            vm(fine, F32),
            vm(fine, F32),
            vm((n_gy, 8, LANES), F32),
            vm((n_gx, 8, LANES), F32),
            vm((3, WIDTH, COARSE), BF16),
            vm((WIDTH, 3 * COARSE), F32),
            vm((WIDTH, POINTS), F32),
            vm((2, WIDTH, 32, LANES), F32),
            vm((2, SLOTS, 32, LANES), F32),
            vm((SUPPORT, SUPPORT, COARSE), BF16),
            dma((12,)),
            dma((2,)),
            dma((2,)),
            dma((2,)),
            dma((2,)),
            dma((8,)),
            dma((8,)),
            dma((n_gy,)),
            dma((n_gy,)),
            dma((n_gx,)),
            dma((n_gx,)),
            dma((3,)),
        ],
        compiler_params=pltpu.CompilerParams(
            collective_id=0, has_side_effects=True, vmem_limit_bytes=62 * 1024 * 1024
        ),
    )(
        rhs.reshape(fine), rhs.reshape(1, 1024), diag.reshape(fine), sup, wts, pin, off,
        cnt.reshape(2, LANES), cf, cs, w1, w2.T,
    )
    return sol.reshape(1024), res.reshape(1024), gram


def solution(mesh):
    both = ("gx", "gy")
    placed = (
        P(both), P(both), P(None, both), P(None, both), P(None, both), P(None, both),
        P(both), P(None, both), P(None, both), P(), P(),
    )
    return jax.shard_map(
        functools.partial(on_device, mesh.shape["gx"], mesh.shape["gy"]),
        mesh=mesh,
        in_specs=placed,
        out_specs=(P(both), P(both), P(None, None, both)),
        check_vma=False,
    )
```

```python
import functools

import jax
import jax.numpy as jnp
from jax import lax
from jax.experimental import pallas as pl
from jax.experimental.pallas import tpu as pltpu
from jax.sharding import PartitionSpec as P

MESH = pl.DeviceIdType.MESH
F32 = jnp.float32
BF16 = jnp.bfloat16
SUPPORT = 27
LANES = 128
ROWS = 8
CLASSES = 17
WINDOW = 24
SLOTS = 16
WIDTH = 32
HIDDEN = 64
COARSE = 256
POINTS = 4096
NT = (((1,), (1,)), ((), ()))
TN = (((0,), (0,)), ((), ()))


def spread_rows(row, shape):
    return jnp.broadcast_to(row, shape)


def kernel(
    n_gx,
    n_gy,
    rhs, rhs_row, diag, sup, wts, pin, off, cnt, cf, cs, w1, w2,
    sol_o, res_o, gram_o,
    row0, diag_v, sup_v, wts_v, pin_v, off_v, cnt_v, cs_v, w1_v, w2_v,
    hi_s, lo_s, lw_s, xw0, xw1, row1, fwd, rabs, shift_s, part, mid1,
    to_left, to_right, from_left, from_right, to_left1, to_right1, from_left1, from_right1,
    ag, agx,
    cfw, table, feats, near, kern,
    in_sem, halo_send, halo_recv, cf_send, cf_recv, ex_send, ex_recv,
    ag_send, ag_recv, agx_send, agx_recv,
):
    gx = lax.axis_index("gx")
    gy = lax.axis_index("gy")
    n = n_gx * n_gy
    block = gx * n_gy + gy

    def device(step):
        other = lax.rem(block + n + step, n)
        return lax.div(other, n_gy), lax.rem(other, n_gy)

    left2, left, right, right2 = device(-2), device(-1), device(1), device(2)

    plane = [(gx, lax.rem(gy + d, n_gy)) for d in range(1, n_gy)]
    column = [(lax.rem(gx + d, n_gx), gy) for d in range(1, n_gx)]

    moves = [
        (rhs, xw0.at[pl.ds(8, 8)]), (cf, cfw.at[1]), (sup, sup_v), (wts, wts_v), (rhs_row, row0), (diag, diag_v),
        (pin, pin_v), (w1, w1_v), (w2, w2_v), (cs, cs_v), (off, off_v), (cnt, cnt_v),
    ]
    copies = [pltpu.make_async_copy(src, dst, in_sem.at[i]) for i, (src, dst) in enumerate(moves)]
    for copy in copies:
        copy.start()

    barrier = pltpu.get_barrier_semaphore()
    for other in (left, right, left2, right2, *plane, *column):
        pl.semaphore_signal(barrier, inc=1, device_id=other, device_id_type=MESH)

    def remote(src, dst, send, recv, device):
        return pltpu.make_async_remote_copy(
            src_ref=src, dst_ref=dst, send_sem=send, recv_sem=recv, device_id=device, device_id_type=MESH
        )

    for i in (0, 1):
        copies[i].wait()
    pl.semaphore_wait(barrier, 4 + len(plane) + len(column))

    started = []

    def arrive(copies):
        for copy in copies:
            copy.wait_recv()
        started.extend(copies)

    halo0 = [
        remote(xw0.at[pl.ds(8, 8)], xw0.at[pl.ds(0, 8)], halo_send.at[0], halo_recv.at[0], right),
        remote(xw0.at[pl.ds(8, 8)], xw0.at[pl.ds(16, 8)], halo_send.at[1], halo_recv.at[1], left),
    ]
    for copy in halo0:
        copy.start()
    cf_halo = [
        remote(cfw.at[1], cfw.at[0], cf_send.at[0], cf_recv.at[0], right),
        remote(cfw.at[1], cfw.at[2], cf_send.at[1], cf_recv.at[1], left),
    ]
    for copy in cf_halo:
        copy.start()

    for i in range(2, 6):
        copies[i].wait()
    lane = lax.broadcasted_iota(jnp.int32, (8, LANES), 1)
    for b in range(4):
        rows = 8 if b < 3 else 3
        for r in range(ROWS):
            at = (slice(8 * b, 8 * b + rows), slice(LANES * r, LANES * (r + 1)))
            value = sup_v[at]
            place = value + lane[:rows]
            live = jnp.where(value >= 0, wts_v[at], 0.0)
            hi = lax.shift_right_arithmetic(place, 7)
            lo = jnp.bitwise_and(place, 127)
            if rows < 8:
                pad = 8 - rows
                at = (slice(8 * b, 8 * b + 8), at[1])
                hi = jnp.concatenate([hi, jnp.full((pad, LANES), -1, jnp.int32)], axis=0)
                lo = jnp.concatenate([lo, jnp.zeros((pad, LANES), jnp.int32)], axis=0)
                live = jnp.concatenate([live, jnp.zeros((pad, LANES), F32)], axis=0)
            hi_s[at] = hi
            lo_s[at] = lo
            lw_s[at] = live

    iota_hi = lax.broadcasted_iota(jnp.int32, (WINDOW, LANES), 0)
    iota_lo = lax.broadcasted_iota(jnp.int32, (LANES, LANES), 0)

    def two_terms(value):
        first = value.astype(BF16).astype(F32)
        return [first, value - first]

    def scatter(field_row, with_abs):
        count = 4 if with_abs else 2

        def step(j, total):
            hi = hi_s[pl.ds(j, 1), :]
            lo = lo_s[pl.ds(j, 1), :]
            w = lw_s[pl.ds(j, 1), :]
            terms = two_terms(w * field_row[...])
            if with_abs:
                terms = terms + two_terms(jnp.abs(w))
            left_parts, ones = [], []
            for r in range(ROWS):
                at = slice(LANES * r, LANES * (r + 1))
                hit = spread_rows(hi[:, at], (WINDOW, LANES)) == iota_hi - r
                left_parts.append(
                    jnp.concatenate(
                        [jnp.where(hit, spread_rows(t[:, at], (WINDOW, LANES)), 0.0) for t in terms], axis=0
                    ).astype(BF16)
                )
                ones.append(
                    jnp.where(spread_rows(lo[:, at], (LANES, LANES)) == iota_lo, 1.0, 0.0).astype(BF16)
                )
            return total + lax.dot_general(
                jnp.concatenate(left_parts, axis=1), jnp.concatenate(ones, axis=1), NT, preferred_element_type=F32
            )

        total = lax.fori_loop(0, SUPPORT, step, jnp.zeros((WINDOW * count, LANES), F32), unroll=9)
        out = [total[:24] + total[24:48]]
        if with_abs:
            out.append(total[48:72] + total[72:96])
        return out

    def forward(window, with_abs):
        def row(r, carry):
            near_rows = [spread_rows(window[pl.ds(r + k, 1), :], (8, LANES)) for k in range(CLASSES)]
            lanes = pl.ds(pl.multiple_of(r * LANES, LANES), LANES)
            total = jnp.zeros((8, LANES), F32)
            weight = jnp.zeros((8, LANES), F32)
            for b in range(4):
                hi = hi_s[8 * b : 8 * b + 8, lanes]
                lo = lo_s[8 * b : 8 * b + 8, lanes]
                w = lw_s[8 * b : 8 * b + 8, lanes]
                got = jnp.zeros((8, LANES), F32)
                for k in range(CLASSES):
                    got = jnp.where(hi == k, jnp.take_along_axis(near_rows[k], lo, axis=1, mode="promise_in_bounds"), got)
                total = total + w * got
                if with_abs:
                    weight = weight + jnp.abs(w)
            fwd[pl.ds(r, 1), :] = jnp.sum(total, axis=0, keepdims=True)
            if with_abs:
                rabs[pl.ds(r, 1), :] = jnp.sum(weight, axis=0, keepdims=True)
            return carry

        lax.fori_loop(0, ROWS, row, 0, unroll=4)

    lane_group = lax.div(lax.broadcasted_iota(jnp.int32, (1, LANES), 1), 32)

    def row_of(*fields):
        row = jnp.zeros((1, LANES), F32)
        for i, field in enumerate(fields):
            part = jnp.sum(field, axis=0, keepdims=True)
            part = part + pltpu.roll(part, 64, 1)
            part = part + pltpu.roll(part, 32, 1)
            row = jnp.where(lane_group == i, part, row)
        return row

    def to_others(slots, me, row, send, recv, others):
        slots[me] = row
        copies = [
            remote(slots.at[me], slots.at[me], send.at[i], recv.at[i], other) for i, other in enumerate(others)
        ]
        for copy in copies:
            copy.start()
        return copies

    def sum_of(slots, copies):
        arrive(copies)
        return jnp.sum(slots[...], axis=0)

    back, size = scatter(row0, True)
    for i in range(6, 12):
        copies[i].wait()

    chunk = 2048

    def mlp(i, carry):
        at = pl.ds(pl.multiple_of(i * chunk, chunk), chunk)
        hidden = lax.dot_general(w1_v[...], pin_v[:, at], TN, preferred_element_type=F32)
        hidden = jnp.maximum(hidden, 0.0).astype(BF16)
        out = jnp.dot(w2_v[...], hidden, preferred_element_type=F32)
        feats[:, at] = out.astype(BF16).astype(F32)
        return carry

    lax.fori_loop(0, POINTS // chunk, mlp, 0)

    arrive(halo0)
    forward(xw0, True)
    r0 = xw0[8:16, :]
    to_left[0:8, :] = back[0:8] + size[0:8] * xw0[0:8, :]
    to_left[8:16, :] = size[0:8]
    to_right[0:8, :] = back[16:24] + size[16:24] * xw0[16:24, :]
    to_right[8:16, :] = size[16:24]
    shift = diag_v[...] + rabs[...] + size[8:16]
    part[...] = shift * r0 + fwd[...] + back[8:16]
    shift_s[...] = shift
    near_by = [
        remote(part, from_left.at[pl.ds(0, 8)], ex_send.at[0], ex_recv.at[0], right),
        remote(part, from_right.at[pl.ds(0, 8)], ex_send.at[1], ex_recv.at[1], left),
        remote(to_right, from_left.at[pl.ds(8, 16)], ex_send.at[2], ex_recv.at[2], right),
        remote(to_left, from_right.at[pl.ds(8, 16)], ex_send.at[3], ex_recv.at[3], left),
        remote(to_right.at[pl.ds(0, 8)], from_left.at[pl.ds(24, 8)], ex_send.at[4], ex_recv.at[4], right2),
        remote(to_left.at[pl.ds(0, 8)], from_right.at[pl.ds(24, 8)], ex_send.at[5], ex_recv.at[5], left2),
    ]
    for copy in near_by:
        copy.start()

    arrive(cf_halo)
    for k in range(6):
        table[WIDTH * k : WIDTH * (k + 1), :] = cfw[k // 2][:, LANES * (k % 2) : LANES * (k % 2 + 1)]
    iota_far = lax.broadcasted_iota(jnp.int32, (LANES, COARSE), 0)

    def support_features(j, carry):
        value = cs_v[pl.ds(j, 1), :]
        hi = spread_rows(lax.shift_right_arithmetic(value, 7), (8, COARSE))
        lo = spread_rows(jnp.bitwise_and(value, 127), (LANES, COARSE))
        ones = jnp.where(lo == iota_far, 1.0, 0.0).astype(BF16)
        got = jnp.dot(table[...], ones, preferred_element_type=F32)
        hits = [hi == k for k in range(6)]
        for q in range(4):
            picked = jnp.zeros((8, COARSE), F32)
            for k in range(6):
                picked = jnp.where(hits[k], got[WIDTH * k + 8 * q : WIDTH * k + 8 * q + 8], picked)
            for c in range(2):
                near[c, pl.ds(32 * 8 * q + j, 8, stride=32), :] = picked[:, LANES * c : LANES * (c + 1)]
        return carry

    lax.fori_loop(0, SUPPORT, support_features, 0, unroll=3)

    iota_j = lax.broadcasted_iota(jnp.int32, (32, LANES), 0)
    tops = jnp.where(iota_j >= 18, 2, jnp.where(iota_j >= 9, 1, 0))
    rest = iota_j - 9 * tops
    middles = jnp.where(rest >= 6, 2, jnp.where(rest >= 3, 1, 0))
    digit = [tops, middles, rest - 3 * middles]
    group = 4

    def kernel_values(i, carry):
        c = lax.rem(i, 2)
        s0 = lax.div(i, 2) * group
        points = [pl.ds(pl.multiple_of((s0 + g) * COARSE + c * LANES, LANES), LANES) for g in range(group)]
        dots = [[jnp.zeros((8, LANES), F32) for _ in range(4)] for _ in range(group)]
        for e in range(WIDTH):
            sources = [near[c, pl.ds(32 * e + 8 * b, 8), :] for b in range(4)]
            for g in range(group):
                feat = spread_rows(feats[e : e + 1, points[g]], (8, LANES))
                dots[g] = [dots[g][b] + feat * sources[b] for b in range(4)]
        counts = cnt_v[pl.ds(c, 1), :]
        for g in range(group):
            factor = jnp.where(s0 + g < counts, WIDTH**-0.5, 0.0)
            product = None
            for a in range(3):
                t = off_v[a : a + 1, points[g]]
                q = [0.5 * (1.0 - t) * (1.0 - t), 0.5 + t - t * t, 0.5 * t * t]
                if a == 0:
                    q = [part * factor for part in q]
                q = [spread_rows(part, (32, LANES)) for part in q]
                value = jnp.where(digit[a] == 0, q[0], jnp.where(digit[a] == 1, q[1], q[2]))
                product = value if product is None else product * value
            for b in range(4):
                kern[c, s0 + g, 8 * b : 8 * b + 8, :] = dots[g][b] * product[8 * b : 8 * b + 8]
        return carry

    lax.fori_loop(0, 2 * SLOTS // group, kernel_values, 0)

    arrive(near_by)
    xw1[0:8, :] = from_left[0:8, :] + to_left[0:8, :] + from_left[24:32, :]
    xw1[8:16, :] = part[...] + from_left[8:16, :] + from_right[8:16, :]
    xw1[16:24, :] = from_right[0:8, :] + to_right[0:8, :] + from_right[24:32, :]
    shift_s[...] = shift_s[...] + (from_left[16:24, :] + from_right[16:24, :])
    forward(xw1, False)
    q0 = xw1[8:16, :]
    first = to_others(ag, gy, row_of(r0 * r0, r0 * q0, q0 * q0, shift_s[...] * (q0 * q0) + 2.0 * q0 * fwd[...]), ag_send, ag_recv, plane)
    for r in range(ROWS):
        row1[0:1, LANES * r : LANES * (r + 1)] = q0[r : r + 1]

    (back,) = scatter(row1, False)
    to_left1[...] = back[0:8]
    to_right1[...] = back[16:24]
    mid1[...] = back[8:16]
    ends = [
        remote(to_right1, from_left1, ex_send.at[6], ex_recv.at[6], right),
        remote(to_left1, from_right1, ex_send.at[7], ex_recv.at[7], left),
    ]
    for copy in ends:
        copy.start()

    second = to_others(agx, gx, sum_of(ag, first), agx_send, agx_recv, column)

    def gram_rows(i, carry):
        c = lax.rem(i, 2)
        j0 = lax.div(i, 2) * 3
        here = pl.ds(pl.multiple_of(c * LANES, LANES), LANES)
        sums = [[jnp.zeros((8, LANES), F32) for _ in range(4)] for _ in range(3)]
        for s in range(SLOTS):
            columns = [kern[c, s, 8 * b : 8 * b + 8, :] for b in range(4)]
            for g in range(3):
                one = spread_rows(kern[c, s, pl.ds(j0 + g, 1), :], (8, LANES))
                sums[g] = [sums[g][b] + one * columns[b] for b in range(4)]
        for g in range(3):
            whole = jnp.concatenate(sums[g], axis=0).astype(BF16)
            gram_o[j0 + g, :, here] = whole[:SUPPORT]
        return carry

    lax.fori_loop(0, 18, gram_rows, 0)
    row = sum_of(agx, second)
    rr0, rq, qq, qaq = [jnp.sum(jnp.where(lane_group == i, row, 0.0), axis=1, keepdims=True) for i in range(4)]
    alpha0 = rr0 / rq
    shear = rq / rr0
    hh = qq - shear * rq
    hah = qaq - 2.0 * shear * qq + shear * shear * rq
    rr1 = alpha0 * alpha0 * hh
    beta = rr1 / rr0
    alpha1 = rr1 / (alpha0 * alpha0 * hah - beta * rr1 * shear)
    arrive(ends)
    r1 = r0 - alpha0 * q0
    image = shift_s[...] * q0 + fwd[...] + (mid1[...] + from_left1[...] + from_right1[...])
    sol_o[...] = alpha0 * r0 + alpha1 * (r1 + beta * r0)
    res_o[...] = r1 - alpha1 * ((1.0 + beta) * q0 - alpha0 * image)
    for copy in started:
        copy.wait_send()


def hand_over(sol, res, gram, sol_o, res_o, gram_o, sem):
    pairs = [(gram, gram_o), (sol, sol_o), (res, res_o)]
    copies = [pltpu.make_async_copy(src, dst, sem.at[i]) for i, (src, dst) in enumerate(pairs)]
    for copy in copies:
        copy.start()
    for copy in copies:
        copy.wait()


def on_device(n_gx, n_gy, rhs, diag, sup, wts, pin, off, cnt, cf, cs, w1, w2):
    vm = pltpu.VMEM
    dma = pltpu.SemaphoreType.DMA
    fine = (ROWS, LANES)
    sol, res, gram = pl.pallas_call(
        functools.partial(kernel, n_gx, n_gy),
        out_shape=[
            pltpu.VMEM(fine, F32),
            pltpu.VMEM(fine, F32),
            pltpu.VMEM((SUPPORT, SUPPORT, COARSE), BF16),
        ],
        in_specs=[pl.BlockSpec(memory_space=pl.ANY)] * 12,
        out_specs=[pl.BlockSpec(memory_space=pltpu.VMEM)] * 3,
        scratch_shapes=[
            vm((1, 1024), F32),
            vm(fine, F32),
            vm((SUPPORT, 1024), jnp.int32),
            vm((SUPPORT, 1024), F32),
            vm((WIDTH, POINTS), BF16),
            vm((3, POINTS), F32),
            vm((2, LANES), jnp.int32),
            vm((SUPPORT, COARSE), jnp.int32),
            vm((WIDTH, HIDDEN), BF16),
            vm((WIDTH, HIDDEN), BF16),
            vm((32, 1024), jnp.int32),
            vm((32, 1024), jnp.int32),
            vm((32, 1024), F32),
            vm((WINDOW, LANES), F32),
            vm((WINDOW, LANES), F32),
            vm((1, 1024), F32),
            vm(fine, F32),
            vm(fine, F32),
            vm(fine, F32),
            vm(fine, F32),
            vm(fine, F32),
            vm((16, LANES), F32),
            vm((16, LANES), F32),
            vm((32, LANES), F32),
            vm((32, LANES), F32),
            vm(fine, F32),
            vm(fine, F32),
            vm(fine, F32),
            vm(fine, F32),
            vm((n_gy, 1, LANES), F32),
            vm((n_gx, 1, LANES), F32),
            vm((3, WIDTH, COARSE), BF16),
            vm((6 * WIDTH, LANES), BF16),
            vm((WIDTH, POINTS), F32),
            vm((2, WIDTH * 32, LANES), F32),
            vm((2, SLOTS, 32, LANES), F32),
            dma((12,)),
            dma((2,)),
            dma((2,)),
            dma((2,)),
            dma((2,)),
            dma((8,)),
            dma((8,)),
            dma((n_gy - 1,)),
            dma((n_gy - 1,)),
            dma((n_gx - 1,)),
            dma((n_gx - 1,)),
        ],
        compiler_params=pltpu.CompilerParams(
            collective_id=0, has_side_effects=True, vmem_limit_bytes=62 * 1024 * 1024
        ),
    )(
        rhs.reshape(fine), rhs.reshape(1, 1024), diag.reshape(fine), sup, wts, pin, off,
        cnt.reshape(2, LANES), cf, cs, w1, w2.T,
    )
    sol, res, gram = pl.pallas_call(
        hand_over,
        out_shape=[
            jax.ShapeDtypeStruct(fine, F32),
            jax.ShapeDtypeStruct(fine, F32),
            jax.ShapeDtypeStruct((SUPPORT, SUPPORT, COARSE), BF16),
        ],
        in_specs=[pl.BlockSpec(memory_space=pl.ANY)] * 3,
        out_specs=[pl.BlockSpec(memory_space=pl.ANY)] * 3,
        scratch_shapes=[dma((3,))],
        compiler_params=pltpu.CompilerParams(vmem_limit_bytes=4 * 1024 * 1024),
    )(sol, res, gram)
    return sol.reshape(1024), res.reshape(1024), gram


def solution(mesh):
    both = ("gx", "gy")
    placed = (
        P(both), P(both), P(None, both), P(None, both), P(None, both), P(None, both),
        P(both), P(None, both), P(None, both), P(), P(),
    )
    return jax.shard_map(
        functools.partial(on_device, mesh.shape["gx"], mesh.shape["gy"]),
        mesh=mesh,
        in_specs=placed,
        out_specs=(P(both), P(both), P(None, None, both)),
        check_vma=False,
    )
```

```python
import functools

import jax
import jax.numpy as jnp
from jax import lax
from jax.experimental import pallas as pl
from jax.experimental.pallas import tpu as pltpu
from jax.sharding import PartitionSpec as P

MESH = pl.DeviceIdType.MESH
F32 = jnp.float32
BF16 = jnp.bfloat16
SUPPORT = 27
LANES = 128
ROWS = 8
CLASSES = 17
WINDOW = 24
SLOTS = 16
WIDTH = 32
HIDDEN = 64
COARSE = 256
POINTS = 4096
NT = (((1,), (1,)), ((), ()))
TN = (((0,), (0,)), ((), ()))


def spread_rows(row, shape):
    return jnp.broadcast_to(row, shape)


def kernel(
    n_gx,
    n_gy,
    rhs, rhs_row, diag, sup, wts, pin, off, cnt, cf, cs, w1, w2,
    sol_o, res_o, gram_o,
    row0, diag_v, sup_v, wts_v, pin_v, off_v, cnt_v, cs_v, w1_v, w2_v,
    hi_s, lo_s, lw_s, xw0, xw1, row1, fwd, rabs, shift_s, part, mid1,
    to_left, to_right, from_left, from_right, to_left1, to_right1, from_left1, from_right1,
    ag, agx,
    cfw, feats, near, kern,
    in_sem, halo_send, halo_recv, cf_send, cf_recv, ex_send, ex_recv,
    ag_send, ag_recv, agx_send, agx_recv,
):
    gx = lax.axis_index("gx")
    gy = lax.axis_index("gy")
    n = n_gx * n_gy
    block = gx * n_gy + gy

    def device(step):
        other = lax.rem(block + n + step, n)
        return lax.div(other, n_gy), lax.rem(other, n_gy)

    left2, left, right, right2 = device(-2), device(-1), device(1), device(2)

    plane = [(gx, lax.rem(gy + d, n_gy)) for d in range(1, n_gy)]
    column = [(lax.rem(gx + d, n_gx), gy) for d in range(1, n_gx)]

    moves = [
        (rhs, xw0.at[pl.ds(8, 8)]), (cf, cfw.at[1]), (sup, sup_v), (wts, wts_v), (rhs_row, row0), (diag, diag_v),
        (pin, pin_v), (w1, w1_v), (w2, w2_v), (cs, cs_v), (off, off_v), (cnt, cnt_v),
    ]
    copies = [pltpu.make_async_copy(src, dst, in_sem.at[i]) for i, (src, dst) in enumerate(moves)]
    copies[0].start()

    barrier = pltpu.get_barrier_semaphore()
    for other in (left, right, left2, right2, *plane, *column):
        pl.semaphore_signal(barrier, inc=1, device_id=other, device_id_type=MESH)
    for copy in copies[1:]:
        copy.start()

    def remote(src, dst, send, recv, device):
        return pltpu.make_async_remote_copy(
            src_ref=src, dst_ref=dst, send_sem=send, recv_sem=recv, device_id=device, device_id_type=MESH
        )

    for i in range(2, 6):
        copies[i].wait()
    lane = lax.broadcasted_iota(jnp.int32, (8, LANES), 1)
    for b in range(4):
        rows = 8 if b < 3 else 3
        for r in range(ROWS):
            at = (slice(8 * b, 8 * b + rows), slice(LANES * r, LANES * (r + 1)))
            value = sup_v[at]
            place = value + lane[:rows]
            live = jnp.where(value >= 0, wts_v[at], 0.0)
            hi = lax.shift_right_arithmetic(place, 7)
            lo = jnp.bitwise_and(place, 127)
            if rows < 8:
                pad = 8 - rows
                at = (slice(8 * b, 8 * b + 8), at[1])
                hi = jnp.concatenate([hi, jnp.full((pad, LANES), -1, jnp.int32)], axis=0)
                lo = jnp.concatenate([lo, jnp.zeros((pad, LANES), jnp.int32)], axis=0)
                live = jnp.concatenate([live, jnp.zeros((pad, LANES), F32)], axis=0)
            hi_s[at] = hi
            lo_s[at] = lo
            lw_s[at] = live

    for i in (0, 1):
        copies[i].wait()
    pl.semaphore_wait(barrier, 4 + len(plane) + len(column))

    started = []

    def arrive(copies):
        for copy in copies:
            copy.wait_recv()
        started.extend(copies)

    halo0 = [
        remote(xw0.at[pl.ds(8, 8)], xw0.at[pl.ds(0, 8)], halo_send.at[0], halo_recv.at[0], right),
        remote(xw0.at[pl.ds(8, 8)], xw0.at[pl.ds(16, 8)], halo_send.at[1], halo_recv.at[1], left),
    ]
    for copy in halo0:
        copy.start()
    cf_halo = [
        remote(cfw.at[1], cfw.at[0], cf_send.at[0], cf_recv.at[0], right),
        remote(cfw.at[1], cfw.at[2], cf_send.at[1], cf_recv.at[1], left),
    ]
    for copy in cf_halo:
        copy.start()

    iota_hi = lax.broadcasted_iota(jnp.int32, (WINDOW, LANES), 0)
    iota_lo = lax.broadcasted_iota(jnp.int32, (LANES, LANES), 0)

    def two_terms(value):
        first = value.astype(BF16).astype(F32)
        return [first, value - first]

    def scatter(field_row, with_abs):
        count = 4 if with_abs else 2

        def step(j, total):
            hi = hi_s[pl.ds(j, 1), :]
            lo = lo_s[pl.ds(j, 1), :]
            w = lw_s[pl.ds(j, 1), :]
            terms = two_terms(w * field_row[...])
            if with_abs:
                terms = terms + two_terms(jnp.abs(w))
            left_parts, ones = [], []
            for r in range(ROWS):
                at = slice(LANES * r, LANES * (r + 1))
                hit = spread_rows(hi[:, at], (WINDOW, LANES)) == iota_hi - r
                left_parts.append(
                    jnp.concatenate(
                        [jnp.where(hit, spread_rows(t[:, at], (WINDOW, LANES)), 0.0) for t in terms], axis=0
                    ).astype(BF16)
                )
                ones.append(
                    jnp.where(spread_rows(lo[:, at], (LANES, LANES)) == iota_lo, 1.0, 0.0).astype(BF16)
                )
            return total + lax.dot_general(
                jnp.concatenate(left_parts, axis=1), jnp.concatenate(ones, axis=1), NT, preferred_element_type=F32
            )

        total = lax.fori_loop(0, SUPPORT, step, jnp.zeros((WINDOW * count, LANES), F32), unroll=9)
        out = [total[:24] + total[24:48]]
        if with_abs:
            out.append(total[48:72] + total[72:96])
        return out

    def forward(window, with_abs):
        def row(r, carry):
            near_rows = [spread_rows(window[pl.ds(r + k, 1), :], (8, LANES)) for k in range(CLASSES)]
            lanes = pl.ds(pl.multiple_of(r * LANES, LANES), LANES)
            total = jnp.zeros((8, LANES), F32)
            weight = jnp.zeros((8, LANES), F32)
            for b in range(4):
                hi = hi_s[8 * b : 8 * b + 8, lanes]
                lo = lo_s[8 * b : 8 * b + 8, lanes]
                w = lw_s[8 * b : 8 * b + 8, lanes]
                got = jnp.zeros((8, LANES), F32)
                for k in range(CLASSES):
                    got = jnp.where(hi == k, jnp.take_along_axis(near_rows[k], lo, axis=1, mode="promise_in_bounds"), got)
                total = total + w * got
                if with_abs:
                    weight = weight + jnp.abs(w)
            fwd[pl.ds(r, 1), :] = jnp.sum(total, axis=0, keepdims=True)
            if with_abs:
                rabs[pl.ds(r, 1), :] = jnp.sum(weight, axis=0, keepdims=True)
            return carry

        lax.fori_loop(0, ROWS, row, 0, unroll=4)

    def tile_of(*fields):
        return jnp.concatenate([jnp.sum(field, axis=0, keepdims=True) for field in fields], axis=0)

    def to_others(slots, me, row, send, recv, others):
        slots[me] = row
        copies = [
            remote(slots.at[me], slots.at[me], send.at[i], recv.at[i], other) for i, other in enumerate(others)
        ]
        for copy in copies:
            copy.start()
        return copies

    def sum_of(slots, copies):
        arrive(copies)
        return jnp.sum(slots[...], axis=0)

    back, size = scatter(row0, True)
    for i in range(6, 12):
        copies[i].wait()

    chunk = 2048

    def mlp(i, carry):
        at = pl.ds(pl.multiple_of(i * chunk, chunk), chunk)
        hidden = lax.dot_general(w1_v[...], pin_v[:, at], TN, preferred_element_type=F32)
        hidden = jnp.maximum(hidden, 0.0).astype(BF16)
        out = jnp.dot(w2_v[...], hidden, preferred_element_type=F32)
        feats[:, at] = out.astype(BF16).astype(F32)
        return carry

    lax.fori_loop(0, POINTS // chunk, mlp, 0)

    arrive(halo0)
    forward(xw0, True)
    r0 = xw0[8:16, :]
    to_left[0:8, :] = back[0:8] + size[0:8] * xw0[0:8, :]
    to_left[8:16, :] = size[0:8]
    to_right[0:8, :] = back[16:24] + size[16:24] * xw0[16:24, :]
    to_right[8:16, :] = size[16:24]
    shift = diag_v[...] + rabs[...] + size[8:16]
    part[...] = shift * r0 + fwd[...] + back[8:16]
    shift_s[...] = shift
    near_by = [
        remote(part, from_left.at[pl.ds(0, 8)], ex_send.at[0], ex_recv.at[0], right),
        remote(part, from_right.at[pl.ds(0, 8)], ex_send.at[1], ex_recv.at[1], left),
        remote(to_right, from_left.at[pl.ds(8, 16)], ex_send.at[2], ex_recv.at[2], right),
        remote(to_left, from_right.at[pl.ds(8, 16)], ex_send.at[3], ex_recv.at[3], left),
        remote(to_right.at[pl.ds(0, 8)], from_left.at[pl.ds(24, 8)], ex_send.at[4], ex_recv.at[4], right2),
        remote(to_left.at[pl.ds(0, 8)], from_right.at[pl.ds(24, 8)], ex_send.at[5], ex_recv.at[5], left2),
    ]
    for copy in near_by:
        copy.start()

    arrive(cf_halo)
    iota_far = lax.broadcasted_iota(jnp.int32, (COARSE, COARSE), 0)

    def support_features(j, carry):
        value = cs_v[pl.ds(j, 1), :]
        side = spread_rows(lax.shift_right_arithmetic(value, 8), (8, COARSE))
        place = spread_rows(jnp.bitwise_and(value, COARSE - 1), (COARSE, COARSE))
        ones = jnp.where(place == iota_far, 1.0, 0.0).astype(BF16)
        got = jnp.dot(cfw[...].reshape(3 * WIDTH, COARSE), ones, preferred_element_type=F32)
        hits = [side == k for k in range(3)]
        for q in range(4):
            picked = jnp.zeros((8, COARSE), F32)
            for k in range(3):
                picked = jnp.where(hits[k], got[WIDTH * k + 8 * q : WIDTH * k + 8 * q + 8], picked)
            for c in range(2):
                near[c, pl.ds(32 * 8 * q + j, 8, stride=32), :] = picked[:, LANES * c : LANES * (c + 1)]
        return carry

    lax.fori_loop(0, SUPPORT, support_features, 0, unroll=3)

    iota_j = lax.broadcasted_iota(jnp.int32, (32, LANES), 0)
    tops = jnp.where(iota_j >= 18, 2, jnp.where(iota_j >= 9, 1, 0))
    rest = iota_j - 9 * tops
    middles = jnp.where(rest >= 6, 2, jnp.where(rest >= 3, 1, 0))
    digit = [tops, middles, rest - 3 * middles]
    group = 4

    def kernel_values(i, carry):
        c = lax.rem(i, 2)
        s0 = lax.div(i, 2) * group
        points = [pl.ds(pl.multiple_of((s0 + g) * COARSE + c * LANES, LANES), LANES) for g in range(group)]
        dots = [[jnp.zeros((8, LANES), F32) for _ in range(4)] for _ in range(group)]
        for e in range(WIDTH):
            sources = [near[c, pl.ds(32 * e + 8 * b, 8), :] for b in range(4)]
            for g in range(group):
                feat = spread_rows(feats[e : e + 1, points[g]], (8, LANES))
                dots[g] = [dots[g][b] + feat * sources[b] for b in range(4)]
        counts = cnt_v[pl.ds(c, 1), :]
        for g in range(group):
            factor = jnp.where(s0 + g < counts, WIDTH**-0.5, 0.0)
            product = None
            for a in range(3):
                t = off_v[a : a + 1, points[g]]
                q = [0.5 * (1.0 - t) * (1.0 - t), 0.5 + t - t * t, 0.5 * t * t]
                if a == 0:
                    q = [part * factor for part in q]
                q = [spread_rows(part, (32, LANES)) for part in q]
                value = jnp.where(digit[a] == 0, q[0], jnp.where(digit[a] == 1, q[1], q[2]))
                product = value if product is None else product * value
            for b in range(4):
                kern[c, s0 + g, 8 * b : 8 * b + 8, :] = dots[g][b] * product[8 * b : 8 * b + 8]
        return carry

    lax.fori_loop(0, SLOTS // group, kernel_values, 0)

    arrive(near_by)
    xw1[0:8, :] = from_left[0:8, :] + to_left[0:8, :] + from_left[24:32, :]
    xw1[8:16, :] = part[...] + from_left[8:16, :] + from_right[8:16, :]
    xw1[16:24, :] = from_right[0:8, :] + to_right[0:8, :] + from_right[24:32, :]
    shift_s[...] = shift_s[...] + (from_left[16:24, :] + from_right[16:24, :])
    forward(xw1, False)
    q0 = xw1[8:16, :]
    first = to_others(ag, gy, tile_of(r0 * r0, r0 * q0, q0 * q0, shift_s[...] * (q0 * q0) + 2.0 * q0 * fwd[...]), ag_send, ag_recv, plane)
    for r in range(ROWS):
        row1[0:1, LANES * r : LANES * (r + 1)] = q0[r : r + 1]

    (back,) = scatter(row1, False)
    to_left1[...] = back[0:8]
    to_right1[...] = back[16:24]
    mid1[...] = back[8:16]
    ends = [
        remote(to_right1, from_left1, ex_send.at[6], ex_recv.at[6], right),
        remote(to_left1, from_right1, ex_send.at[7], ex_recv.at[7], left),
    ]
    for copy in ends:
        copy.start()

    second = to_others(agx, gx, sum_of(ag, first), agx_send, agx_recv, column)

    lax.fori_loop(SLOTS // group, 2 * SLOTS // group, kernel_values, 0)

    def gram_rows(i, carry):
        c = lax.rem(i, 2)
        j0 = lax.div(i, 2) * 3
        here = pl.ds(pl.multiple_of(c * LANES, LANES), LANES)
        sums = [[jnp.zeros((8, LANES), F32) for _ in range(4)] for _ in range(3)]
        for s in range(SLOTS):
            columns = [kern[c, s, 8 * b : 8 * b + 8, :] for b in range(4)]
            for g in range(3):
                one = spread_rows(kern[c, s, pl.ds(j0 + g, 1), :], (8, LANES))
                sums[g] = [sums[g][b] + one * columns[b] for b in range(4)]
        for g in range(3):
            whole = jnp.concatenate(sums[g], axis=0).astype(BF16)
            gram_o[j0 + g, :, here] = whole[:SUPPORT]
        return carry

    lax.fori_loop(0, 18, gram_rows, 0)
    tile = sum_of(agx, second)
    rr, rq, qq, qaq = [tile[i : i + 1] for i in range(4)]

    def over_lanes(value):
        return jnp.sum(value, axis=1, keepdims=True)

    rr0 = over_lanes(rr)
    alpha0 = rr0 / over_lanes(rq)
    rr1 = over_lanes(rr - alpha0 * (2.0 * rq - alpha0 * qq))
    rar1 = over_lanes(rq - alpha0 * (2.0 * qq - alpha0 * qaq))
    beta = rr1 / rr0
    alpha1 = rr1 / (rar1 - beta * rr1 / alpha0)
    arrive(ends)
    r1 = r0 - alpha0 * q0
    image = shift_s[...] * q0 + fwd[...] + (mid1[...] + from_left1[...] + from_right1[...])
    sol_o[...] = alpha0 * r0 + alpha1 * (r1 + beta * r0)
    res_o[...] = r1 - alpha1 * ((1.0 + beta) * q0 - alpha0 * image)
    for copy in started:
        copy.wait_send()


def hand_over(sol, res, gram, sol_o, res_o, gram_o, sem):
    pairs = [(gram, gram_o), (sol, sol_o), (res, res_o)]
    copies = [pltpu.make_async_copy(src, dst, sem.at[i]) for i, (src, dst) in enumerate(pairs)]
    for copy in copies:
        copy.start()
    for copy in copies:
        copy.wait()


def on_device(n_gx, n_gy, rhs, diag, sup, wts, pin, off, cnt, cf, cs, w1, w2):
    vm = pltpu.VMEM
    dma = pltpu.SemaphoreType.DMA
    fine = (ROWS, LANES)
    sol, res, gram = pl.pallas_call(
        functools.partial(kernel, n_gx, n_gy),
        out_shape=[
            pltpu.VMEM(fine, F32),
            pltpu.VMEM(fine, F32),
            pltpu.VMEM((SUPPORT, SUPPORT, COARSE), BF16),
        ],
        in_specs=[pl.BlockSpec(memory_space=pl.ANY)] * 12,
        out_specs=[pl.BlockSpec(memory_space=pltpu.VMEM)] * 3,
        scratch_shapes=[
            vm((1, 1024), F32),
            vm(fine, F32),
            vm((SUPPORT, 1024), jnp.int32),
            vm((SUPPORT, 1024), F32),
            vm((WIDTH, POINTS), BF16),
            vm((3, POINTS), F32),
            vm((2, LANES), jnp.int32),
            vm((SUPPORT, COARSE), jnp.int32),
            vm((WIDTH, HIDDEN), BF16),
            vm((WIDTH, HIDDEN), BF16),
            vm((32, 1024), jnp.int32),
            vm((32, 1024), jnp.int32),
            vm((32, 1024), F32),
            vm((WINDOW, LANES), F32),
            vm((WINDOW, LANES), F32),
            vm((1, 1024), F32),
            vm(fine, F32),
            vm(fine, F32),
            vm(fine, F32),
            vm(fine, F32),
            vm(fine, F32),
            vm((16, LANES), F32),
            vm((16, LANES), F32),
            vm((32, LANES), F32),
            vm((32, LANES), F32),
            vm(fine, F32),
            vm(fine, F32),
            vm(fine, F32),
            vm(fine, F32),
            vm((n_gy, 4, LANES), F32),
            vm((n_gx, 4, LANES), F32),
            vm((3, WIDTH, COARSE), BF16),
            vm((WIDTH, POINTS), F32),
            vm((2, WIDTH * 32, LANES), F32),
            vm((2, SLOTS, 32, LANES), F32),
            dma((12,)),
            dma((2,)),
            dma((2,)),
            dma((2,)),
            dma((2,)),
            dma((8,)),
            dma((8,)),
            dma((n_gy - 1,)),
            dma((n_gy - 1,)),
            dma((n_gx - 1,)),
            dma((n_gx - 1,)),
        ],
        compiler_params=pltpu.CompilerParams(
            collective_id=0, has_side_effects=True, vmem_limit_bytes=62 * 1024 * 1024
        ),
    )(
        rhs.reshape(fine), rhs.reshape(1, 1024), diag.reshape(fine), sup, wts, pin, off,
        cnt.reshape(2, LANES), cf, cs, w1, w2.T,
    )
    sol, res, gram = pl.pallas_call(
        hand_over,
        out_shape=[
            jax.ShapeDtypeStruct(fine, F32),
            jax.ShapeDtypeStruct(fine, F32),
            jax.ShapeDtypeStruct((SUPPORT, SUPPORT, COARSE), BF16),
        ],
        in_specs=[pl.BlockSpec(memory_space=pl.ANY)] * 3,
        out_specs=[pl.BlockSpec(memory_space=pl.ANY)] * 3,
        scratch_shapes=[dma((3,))],
        compiler_params=pltpu.CompilerParams(vmem_limit_bytes=4 * 1024 * 1024),
    )(sol, res, gram)
    return sol.reshape(1024), res.reshape(1024), gram


def solution(mesh):
    both = ("gx", "gy")
    placed = (
        P(both), P(both), P(None, both), P(None, both), P(None, both), P(None, both),
        P(both), P(None, both), P(None, both), P(), P(),
    )
    return jax.shard_map(
        functools.partial(on_device, mesh.shape["gx"], mesh.shape["gy"]),
        mesh=mesh,
        in_specs=placed,
        out_specs=(P(both), P(both), P(None, None, both)),
        check_vma=False,
    )
```

```python
import functools

import jax
import jax.numpy as jnp
from jax import lax
from jax.experimental import pallas as pl
from jax.experimental.pallas import tpu as pltpu
from jax.sharding import PartitionSpec as P

MESH = pl.DeviceIdType.MESH
F32 = jnp.float32
BF16 = jnp.bfloat16
SUPPORT = 27
LANES = 128
ROWS = 8
CLASSES = 17
WINDOW = 24
SLOTS = 16
WIDTH = 32
HIDDEN = 64
COARSE = 256
POINTS = 4096
NT = (((1,), (1,)), ((), ()))
TN = (((0,), (0,)), ((), ()))


def spread_rows(row, shape):
    return jnp.broadcast_to(row, shape)


def kernel(
    n_gx,
    n_gy,
    rhs, rhs_row, diag, sup, wts, pin, off, cnt, cf, cs, w1, w2,
    sol_o, res_o, gram_o,
    row0, diag_v, sup_v, wts_v, pin_v, off_v, cnt_v, cs_v, w1_v, w2_v,
    hi_s, lo_s, lw_s, xw0, xw1, row1, fwd, rabs, shift_s, part, mid1,
    to_left, to_right, from_left, from_right, to_left1, to_right1, from_left1, from_right1,
    ag, agx,
    cfw, feats, near, kern,
    in_sem, halo_send, halo_recv, cf_send, cf_recv, ex_send, ex_recv,
    ag_send, ag_recv, agx_send, agx_recv,
):
    gx = lax.axis_index("gx")
    gy = lax.axis_index("gy")
    n = n_gx * n_gy
    block = gx * n_gy + gy

    def device(step):
        other = lax.rem(block + n + step, n)
        return lax.div(other, n_gy), lax.rem(other, n_gy)

    left2, left, right, right2 = device(-2), device(-1), device(1), device(2)

    def hops(count, inner):
        def key(d):
            outer, low = divmod(d, inner)
            return -min(outer, count // inner - outer) - min(low, inner - low)

        return sorted(range(1, count), key=key)

    plane = [(gx, lax.rem(gy + d, n_gy)) for d in hops(n_gy, 4)]
    column = [(lax.rem(gx + d, n_gx), gy) for d in hops(n_gx, 2)]

    moves = [
        (rhs, xw0.at[pl.ds(8, 8)]), (cf, cfw.at[1]), (sup, sup_v), (wts, wts_v), (rhs_row, row0), (diag, diag_v),
        (pin, pin_v), (w1, w1_v), (w2, w2_v), (cs, cs_v), (off, off_v), (cnt, cnt_v),
    ]
    copies = [pltpu.make_async_copy(src, dst, in_sem.at[i]) for i, (src, dst) in enumerate(moves)]
    copies[0].start()

    barrier = pltpu.get_barrier_semaphore()
    for other in (left, right, left2, right2, *plane, *column):
        pl.semaphore_signal(barrier, inc=1, device_id=other, device_id_type=MESH)
    for copy in copies[1:]:
        copy.start()

    def remote(src, dst, send, recv, device):
        return pltpu.make_async_remote_copy(
            src_ref=src, dst_ref=dst, send_sem=send, recv_sem=recv, device_id=device, device_id_type=MESH
        )

    for i in range(2, 6):
        copies[i].wait()
    lane = lax.broadcasted_iota(jnp.int32, (8, LANES), 1)
    for b in range(4):
        rows = 8 if b < 3 else 3
        for r in range(ROWS):
            at = (slice(8 * b, 8 * b + rows), slice(LANES * r, LANES * (r + 1)))
            value = sup_v[at]
            place = value + lane[:rows]
            live = jnp.where(value >= 0, wts_v[at], 0.0)
            hi = lax.shift_right_arithmetic(place, 7)
            lo = jnp.bitwise_and(place, 127)
            if rows < 8:
                pad = 8 - rows
                at = (slice(8 * b, 8 * b + 8), at[1])
                hi = jnp.concatenate([hi, jnp.full((pad, LANES), -1, jnp.int32)], axis=0)
                lo = jnp.concatenate([lo, jnp.zeros((pad, LANES), jnp.int32)], axis=0)
                live = jnp.concatenate([live, jnp.zeros((pad, LANES), F32)], axis=0)
            hi_s[at] = hi
            lo_s[at] = lo
            lw_s[at] = live

    for i in (0, 1):
        copies[i].wait()
    pl.semaphore_wait(barrier, 4 + len(plane) + len(column))

    started = []

    def arrive(copies):
        for copy in copies:
            copy.wait_recv()
        started.extend(copies)

    halo0 = [
        remote(rhs, xw0.at[pl.ds(0, 8)], halo_send.at[0], halo_recv.at[0], right),
        remote(rhs, xw0.at[pl.ds(16, 8)], halo_send.at[1], halo_recv.at[1], left),
    ]
    for copy in halo0:
        copy.start()
    cf_halo = [
        remote(cfw.at[1], cfw.at[0], cf_send.at[0], cf_recv.at[0], right),
        remote(cfw.at[1], cfw.at[2], cf_send.at[1], cf_recv.at[1], left),
    ]
    for copy in cf_halo:
        copy.start()

    iota_hi = lax.broadcasted_iota(jnp.int32, (WINDOW, LANES), 0)
    iota_lo = lax.broadcasted_iota(jnp.int32, (LANES, LANES), 0)

    def two_terms(value):
        first = value.astype(BF16).astype(F32)
        return [first, value - first]

    def scatter(field_row, with_abs):
        count = 4 if with_abs else 2

        def step(j, total):
            hi = hi_s[pl.ds(j, 1), :]
            lo = lo_s[pl.ds(j, 1), :]
            w = lw_s[pl.ds(j, 1), :]
            terms = two_terms(w * field_row[...])
            if with_abs:
                terms = terms + two_terms(jnp.abs(w))
            left_parts, ones = [], []
            for r in range(ROWS):
                at = slice(LANES * r, LANES * (r + 1))
                hit = spread_rows(hi[:, at], (WINDOW, LANES)) == iota_hi - r
                left_parts.append(
                    jnp.concatenate(
                        [jnp.where(hit, spread_rows(t[:, at], (WINDOW, LANES)), 0.0) for t in terms], axis=0
                    ).astype(BF16)
                )
                ones.append(
                    jnp.where(spread_rows(lo[:, at], (LANES, LANES)) == iota_lo, 1.0, 0.0).astype(BF16)
                )
            return total + lax.dot_general(
                jnp.concatenate(left_parts, axis=1), jnp.concatenate(ones, axis=1), NT, preferred_element_type=F32
            )

        total = lax.fori_loop(0, SUPPORT, step, jnp.zeros((WINDOW * count, LANES), F32), unroll=9)
        out = [total[:24] + total[24:48]]
        if with_abs:
            out.append(total[48:72] + total[72:96])
        return out

    def forward(window, with_abs):
        def row(r, carry):
            near_rows = [spread_rows(window[pl.ds(r + k, 1), :], (8, LANES)) for k in range(CLASSES)]
            lanes = pl.ds(pl.multiple_of(r * LANES, LANES), LANES)
            total = jnp.zeros((8, LANES), F32)
            weight = jnp.zeros((8, LANES), F32)
            for b in range(4):
                hi = hi_s[8 * b : 8 * b + 8, lanes]
                lo = lo_s[8 * b : 8 * b + 8, lanes]
                w = lw_s[8 * b : 8 * b + 8, lanes]
                got = jnp.zeros((8, LANES), F32)
                for k in range(CLASSES):
                    got = jnp.where(hi == k, jnp.take_along_axis(near_rows[k], lo, axis=1, mode="promise_in_bounds"), got)
                total = total + w * got
                if with_abs:
                    weight = weight + jnp.abs(w)
            fwd[pl.ds(r, 1), :] = jnp.sum(total, axis=0, keepdims=True)
            if with_abs:
                rabs[pl.ds(r, 1), :] = jnp.sum(weight, axis=0, keepdims=True)
            return carry

        lax.fori_loop(0, ROWS, row, 0, unroll=4)

    def tile_of(*fields):
        return jnp.concatenate([jnp.sum(field, axis=0, keepdims=True) for field in fields], axis=0)

    def to_others(slots, me, row, send, recv, others):
        slots[me] = row
        copies = [
            remote(slots.at[me], slots.at[me], send.at[i], recv.at[i], other) for i, other in enumerate(others)
        ]
        for copy in copies:
            copy.start()
        return copies

    def sum_of(slots, copies):
        arrive(copies)
        return jnp.sum(slots[...], axis=0)

    back, size = scatter(row0, True)
    for i in range(6, 12):
        copies[i].wait()

    chunk = 2048

    def mlp(i, carry):
        at = pl.ds(pl.multiple_of(i * chunk, chunk), chunk)
        hidden = lax.dot_general(w1_v[...], pin_v[:, at], TN, preferred_element_type=F32)
        hidden = jnp.maximum(hidden, 0.0).astype(BF16)
        out = jnp.dot(w2_v[...], hidden, preferred_element_type=F32)
        feats[:, at] = out.astype(BF16).astype(F32)
        return carry

    lax.fori_loop(0, POINTS // chunk, mlp, 0)

    arrive(halo0)
    forward(xw0, True)
    r0 = xw0[8:16, :]
    to_left[0:8, :] = back[0:8] + size[0:8] * xw0[0:8, :]
    to_left[8:16, :] = size[0:8]
    to_right[0:8, :] = back[16:24] + size[16:24] * xw0[16:24, :]
    to_right[8:16, :] = size[16:24]
    shift = diag_v[...] + rabs[...] + size[8:16]
    part[...] = shift * r0 + fwd[...] + back[8:16]
    shift_s[...] = shift
    near_by = [
        remote(part, from_left.at[pl.ds(0, 8)], ex_send.at[0], ex_recv.at[0], right),
        remote(part, from_right.at[pl.ds(0, 8)], ex_send.at[1], ex_recv.at[1], left),
        remote(to_right, from_left.at[pl.ds(8, 16)], ex_send.at[2], ex_recv.at[2], right),
        remote(to_left, from_right.at[pl.ds(8, 16)], ex_send.at[3], ex_recv.at[3], left),
        remote(to_right.at[pl.ds(0, 8)], from_left.at[pl.ds(24, 8)], ex_send.at[4], ex_recv.at[4], right2),
        remote(to_left.at[pl.ds(0, 8)], from_right.at[pl.ds(24, 8)], ex_send.at[5], ex_recv.at[5], left2),
    ]
    for copy in near_by:
        copy.start()

    arrive(cf_halo)
    iota_far = lax.broadcasted_iota(jnp.int32, (COARSE, COARSE), 0)

    def support_features(j, carry):
        value = cs_v[pl.ds(j, 1), :]
        side = spread_rows(lax.shift_right_arithmetic(value, 8), (8, COARSE))
        place = spread_rows(jnp.bitwise_and(value, COARSE - 1), (COARSE, COARSE))
        ones = jnp.where(place == iota_far, 1.0, 0.0).astype(BF16)
        got = jnp.dot(cfw[...].reshape(3 * WIDTH, COARSE), ones, preferred_element_type=F32)
        hits = [side == k for k in range(3)]
        for q in range(4):
            picked = jnp.zeros((8, COARSE), F32)
            for k in range(3):
                picked = jnp.where(hits[k], got[WIDTH * k + 8 * q : WIDTH * k + 8 * q + 8], picked)
            for c in range(2):
                near[c, pl.ds(32 * 8 * q + j, 8, stride=32), :] = picked[:, LANES * c : LANES * (c + 1)]
        return carry

    lax.fori_loop(0, SUPPORT, support_features, 0, unroll=3)

    iota_j = lax.broadcasted_iota(jnp.int32, (32, LANES), 0)
    tops = jnp.where(iota_j >= 18, 2, jnp.where(iota_j >= 9, 1, 0))
    rest = iota_j - 9 * tops
    middles = jnp.where(rest >= 6, 2, jnp.where(rest >= 3, 1, 0))
    digit = [tops, middles, rest - 3 * middles]
    group = 4

    def kernel_values(i, carry):
        c = lax.rem(i, 2)
        s0 = lax.div(i, 2) * group
        points = [pl.ds(pl.multiple_of((s0 + g) * COARSE + c * LANES, LANES), LANES) for g in range(group)]
        dots = [[jnp.zeros((8, LANES), F32) for _ in range(4)] for _ in range(group)]
        for e in range(WIDTH):
            sources = [near[c, pl.ds(32 * e + 8 * b, 8), :] for b in range(4)]
            for g in range(group):
                feat = spread_rows(feats[e : e + 1, points[g]], (8, LANES))
                dots[g] = [dots[g][b] + feat * sources[b] for b in range(4)]
        counts = cnt_v[pl.ds(c, 1), :]
        for g in range(group):
            factor = jnp.where(s0 + g < counts, WIDTH**-0.5, 0.0)
            product = None
            for a in range(3):
                t = off_v[a : a + 1, points[g]]
                q = [0.5 * (1.0 - t) * (1.0 - t), 0.5 + t - t * t, 0.5 * t * t]
                if a == 0:
                    q = [part * factor for part in q]
                q = [spread_rows(part, (32, LANES)) for part in q]
                value = jnp.where(digit[a] == 0, q[0], jnp.where(digit[a] == 1, q[1], q[2]))
                product = value if product is None else product * value
            for b in range(4):
                kern[c, s0 + g, 8 * b : 8 * b + 8, :] = dots[g][b] * product[8 * b : 8 * b + 8]
        return carry

    lax.fori_loop(0, SLOTS // group, kernel_values, 0)

    arrive(near_by)
    xw1[0:8, :] = from_left[0:8, :] + to_left[0:8, :] + from_left[24:32, :]
    xw1[8:16, :] = part[...] + from_left[8:16, :] + from_right[8:16, :]
    xw1[16:24, :] = from_right[0:8, :] + to_right[0:8, :] + from_right[24:32, :]
    shift_s[...] = shift_s[...] + (from_left[16:24, :] + from_right[16:24, :])
    forward(xw1, False)
    q0 = xw1[8:16, :]
    first = to_others(ag, gy, tile_of(r0 * r0, r0 * q0, q0 * q0, shift_s[...] * (q0 * q0) + 2.0 * q0 * fwd[...]), ag_send, ag_recv, plane)
    for r in range(ROWS):
        row1[0:1, LANES * r : LANES * (r + 1)] = q0[r : r + 1]

    (back,) = scatter(row1, False)
    to_left1[...] = back[0:8]
    to_right1[...] = back[16:24]
    mid1[...] = back[8:16]
    ends = [
        remote(to_right1, from_left1, ex_send.at[6], ex_recv.at[6], right),
        remote(to_left1, from_right1, ex_send.at[7], ex_recv.at[7], left),
    ]
    for copy in ends:
        copy.start()

    second = to_others(agx, gx, sum_of(ag, first), agx_send, agx_recv, column)

    lax.fori_loop(SLOTS // group, 2 * SLOTS // group, kernel_values, 0)

    def gram_rows(i, carry):
        c = lax.rem(i, 2)
        j0 = lax.div(i, 2) * 3
        here = pl.ds(pl.multiple_of(c * LANES, LANES), LANES)
        sums = [[jnp.zeros((8, LANES), F32) for _ in range(4)] for _ in range(3)]
        for s in range(SLOTS):
            columns = [kern[c, s, 8 * b : 8 * b + 8, :] for b in range(4)]
            for g in range(3):
                one = spread_rows(kern[c, s, pl.ds(j0 + g, 1), :], (8, LANES))
                sums[g] = [sums[g][b] + one * columns[b] for b in range(4)]
        for g in range(3):
            whole = jnp.concatenate(sums[g], axis=0).astype(BF16)
            gram_o[j0 + g, :, here] = whole[:SUPPORT]
        return carry

    lax.fori_loop(0, 18, gram_rows, 0)
    tile = sum_of(agx, second)
    rr, rq, qq, qaq = [tile[i : i + 1] for i in range(4)]

    def over_lanes(value):
        return jnp.sum(value, axis=1, keepdims=True)

    rr0 = over_lanes(rr)
    alpha0 = rr0 / over_lanes(rq)
    rr1 = over_lanes(rr - alpha0 * (2.0 * rq - alpha0 * qq))
    rar1 = over_lanes(rq - alpha0 * (2.0 * qq - alpha0 * qaq))
    beta = rr1 / rr0
    alpha1 = rr1 / (rar1 - beta * rr1 / alpha0)
    arrive(ends)
    r1 = r0 - alpha0 * q0
    image = shift_s[...] * q0 + fwd[...] + (mid1[...] + from_left1[...] + from_right1[...])
    sol_o[...] = alpha0 * r0 + alpha1 * (r1 + beta * r0)
    res_o[...] = r1 - alpha1 * ((1.0 + beta) * q0 - alpha0 * image)
    for copy in started:
        copy.wait_send()


def hand_over(sol, res, gram, sol_o, res_o, gram_o, sem):
    pairs = [(gram, gram_o), (sol, sol_o), (res, res_o)]
    copies = [pltpu.make_async_copy(src, dst, sem.at[i]) for i, (src, dst) in enumerate(pairs)]
    for copy in copies:
        copy.start()
    for copy in copies:
        copy.wait()


def on_device(n_gx, n_gy, rhs, diag, sup, wts, pin, off, cnt, cf, cs, w1, w2):
    vm = pltpu.VMEM
    dma = pltpu.SemaphoreType.DMA
    fine = (ROWS, LANES)
    sol, res, gram = pl.pallas_call(
        functools.partial(kernel, n_gx, n_gy),
        out_shape=[
            pltpu.VMEM(fine, F32),
            pltpu.VMEM(fine, F32),
            pltpu.VMEM((SUPPORT, SUPPORT, COARSE), BF16),
        ],
        in_specs=[pl.BlockSpec(memory_space=pl.ANY)] * 12,
        out_specs=[pl.BlockSpec(memory_space=pltpu.VMEM)] * 3,
        scratch_shapes=[
            vm((1, 1024), F32),
            vm(fine, F32),
            vm((SUPPORT, 1024), jnp.int32),
            vm((SUPPORT, 1024), F32),
            vm((WIDTH, POINTS), BF16),
            vm((3, POINTS), F32),
            vm((2, LANES), jnp.int32),
            vm((SUPPORT, COARSE), jnp.int32),
            vm((WIDTH, HIDDEN), BF16),
            vm((WIDTH, HIDDEN), BF16),
            vm((32, 1024), jnp.int32),
            vm((32, 1024), jnp.int32),
            vm((32, 1024), F32),
            vm((WINDOW, LANES), F32),
            vm((WINDOW, LANES), F32),
            vm((1, 1024), F32),
            vm(fine, F32),
            vm(fine, F32),
            vm(fine, F32),
            vm(fine, F32),
            vm(fine, F32),
            vm((16, LANES), F32),
            vm((16, LANES), F32),
            vm((32, LANES), F32),
            vm((32, LANES), F32),
            vm(fine, F32),
            vm(fine, F32),
            vm(fine, F32),
            vm(fine, F32),
            vm((n_gy, 4, LANES), F32),
            vm((n_gx, 4, LANES), F32),
            vm((3, WIDTH, COARSE), BF16),
            vm((WIDTH, POINTS), F32),
            vm((2, WIDTH * 32, LANES), F32),
            vm((2, SLOTS, 32, LANES), F32),
            dma((12,)),
            dma((2,)),
            dma((2,)),
            dma((2,)),
            dma((2,)),
            dma((8,)),
            dma((8,)),
            dma((n_gy - 1,)),
            dma((n_gy - 1,)),
            dma((n_gx - 1,)),
            dma((n_gx - 1,)),
        ],
        compiler_params=pltpu.CompilerParams(
            collective_id=0, has_side_effects=True, vmem_limit_bytes=62 * 1024 * 1024
        ),
    )(
        rhs.reshape(fine), rhs.reshape(1, 1024), diag.reshape(fine), sup, wts, pin, off,
        cnt.reshape(2, LANES), cf, cs, w1, w2.T,
    )
    sol, res, gram = pl.pallas_call(
        hand_over,
        out_shape=[
            jax.ShapeDtypeStruct(fine, F32),
            jax.ShapeDtypeStruct(fine, F32),
            jax.ShapeDtypeStruct((SUPPORT, SUPPORT, COARSE), BF16),
        ],
        in_specs=[pl.BlockSpec(memory_space=pl.ANY)] * 3,
        out_specs=[pl.BlockSpec(memory_space=pl.ANY)] * 3,
        scratch_shapes=[dma((3,))],
        compiler_params=pltpu.CompilerParams(vmem_limit_bytes=4 * 1024 * 1024),
    )(sol, res, gram)
    return sol.reshape(1024), res.reshape(1024), gram


def solution(mesh):
    both = ("gx", "gy")
    placed = (
        P(both), P(both), P(None, both), P(None, both), P(None, both), P(None, both),
        P(both), P(None, both), P(None, both), P(), P(),
    )
    return jax.shard_map(
        functools.partial(on_device, mesh.shape["gx"], mesh.shape["gy"]),
        mesh=mesh,
        in_specs=placed,
        out_specs=(P(both), P(both), P(None, None, both)),
        check_vma=False,
    )
```
